32 devices in a mesh: group: 2 (over x), member: 16 (over z, y, core).
Axes of the slice: x: 2, y: 2, z: 4, core: 2. Of those that a mesh axis runs over, the one named last changes fastest.
Arguments:
- features: bfloat16 [8192, 256], P(('group', 'member')), may hold values from -6 to 6
- neighbours: int32 [8192, 10], P(('group', 'member')), may hold values from 0 to 639
- send_rows: int32 [512, 16], P(('group', 'member')), may hold values from 0 to 255
- block_counts: int32 [512], P(('group', 'member')), may hold values from 1 to 16, as said below
- hub_rows: int32 [32, 4], P(('group', 'member')), may hold values from 0 to 255
- w_self: bfloat16 [256, 256], replicated, may hold values from -0.375 to 0.375
- w_nbr: bfloat16 [256, 256], replicated, may hold values from -0.375 to 0.375
- cotangent: bfloat16 [8192, 256], P(('group', 'member')), may hold values from -6 to 6
Outputs:
- grad_self: float32 [256, 256], replicated
- grad_nbr: float32 [256, 256], replicated
- grad_features: bfloat16 [8192, 256], P(('group', 'member'))
The draws below stay inside these ranges and needn't reach their ends.
Inputs may be any that keep to these rules, and one draw needn't show every extreme that they name: `block_counts`: entry pair of every fourth pair (pair % 4 == 0) is exactly 16.
All inputs are finite; a program needn't handle non-finite values.
Results may differ from the reference program's by a relative error of at most 0.005.
Values may be sent and summed in bfloat16 or wider, within the bound.
A program may use at most 64 MiB of HBM per device.

```python
import math
import jax
import jax.numpy as jnp

D = 256
NODE_DEV = 256
FANOUT = 10
BLOCK = 16
HUB_DEV = 4
NODES = 8192
OWNERS = 32
SENDS = 512
TABLE = 640
N_GROUP = 2
N_MEMBER = 16


def draw_block_counts(key, part):
    key = jax.random.fold_in(key, 7)
    drawn = jax.random.randint(key, (SENDS,), 1, BLOCK + 1)
    return jnp.where(jnp.arange(SENDS) % 4 == 0, BLOCK, drawn).astype(jnp.int32)


def draw_neighbours(key, part):
    key = jax.random.fold_in(key, 11)
    shape = (NODES, FANOUT)
    kind_key, local_key, border_key, pick_key, far_key, hub_key = jax.random.split(key, 6)
    kind = jax.random.randint(kind_key, shape, 0, 3)
    local_pick = jax.random.randint(local_key, shape, 0, NODE_DEV)
    border_pick = NODE_DEV + jax.random.randint(border_key, shape, 0, N_MEMBER * BLOCK)
    device = (jnp.arange(NODES, dtype=jnp.int32) // NODE_DEV)[:, None]
    partner = jax.random.randint(pick_key, shape, 0, 4)
    anywhere = jax.random.randint(far_key, shape, 0, OWNERS)
    offset = jnp.where(partner == 0, OWNERS // 2, jnp.where(partner == 1, 1, jnp.where(partner == 2, OWNERS - 1, anywhere)))
    owner = (device + offset) % OWNERS
    hub_slot = jax.random.randint(hub_key, shape, 0, HUB_DEV)
    hub_pick = NODE_DEV + N_MEMBER * BLOCK + owner * HUB_DEV + hub_slot
    chosen = jnp.where(kind == 0, local_pick, jnp.where(kind == 1, border_pick, hub_pick))
    chosen = chosen.at[0, 0].set(0)
    chosen = chosen.at[1, 0].set(TABLE - 1)
    return chosen.astype(jnp.int32)


def set_ends(result, rng, least, top_value):
    place = [jax.random.randint(jax.random.fold_in(rng, axis), (), 0, length) for axis, length in enumerate(result.shape)]
    longest = result.shape.index(max(result.shape))
    beside = place[:longest] + [(place[longest] + 1) % result.shape[longest]] + place[longest + 1:]
    return result.at[tuple(place)].set(least).at[tuple(beside)].set(top_value)


def block_scale(key, dims, pieces, smallest, largest):
    gain = 1.0
    for dim, blocks in pieces:
        steps = jax.random.uniform(jax.random.fold_in(jax.random.fold_in(key, 6), dim), (blocks,), jnp.float32, smallest / len(pieces), largest / len(pieces))
        gain = gain * jnp.repeat(jnp.exp(steps), dims[dim] // blocks).reshape((-1,) + (1,) * (len(dims) - 1 - dim))
    return gain


def scatter_about(rng, dims, scale, reach, shards=(), held_as=jnp.bfloat16):
    factor_of = block_scale(rng, dims, shards, -0.22, 0.18) if shards else 1.0
    array = jax.random.normal(rng, dims, jnp.float32) * scale * factor_of
    return jnp.minimum(jnp.maximum(array, -reach), reach).astype(held_as)


def setup_inputs(seed: int = 0) -> dict:
    streams_of = jax.random.split(jax.random.key(seed), 9)
    features = scatter_about(streams_of[0], (NODES, D), 1.0, 6.0, ((0, 32),))
    neighbours = draw_neighbours(jax.random.fold_in(streams_of[8], 71), 0)
    send_rows = set_ends(jax.random.randint(streams_of[2], (SENDS, BLOCK), 0, NODE_DEV), jax.random.fold_in(streams_of[2], 1), 0, NODE_DEV - 1).astype(jnp.int32)
    block_counts = draw_block_counts(jax.random.fold_in(streams_of[8], 71), 0)
    hub_rows = set_ends(jax.random.randint(streams_of[4], (OWNERS, HUB_DEV), 0, NODE_DEV), jax.random.fold_in(streams_of[4], 1), 0, NODE_DEV - 1).astype(jnp.int32)
    w_self = scatter_about(streams_of[5], (D, D), D ** -0.5, 0.375)
    w_nbr = scatter_about(streams_of[6], (D, D), D ** -0.5, 0.375)
    cotangent = scatter_about(streams_of[7], (NODES, D), 1.0, 6.0, ((0, 32),))
    return dict(features=features, neighbours=neighbours, send_rows=send_rows, block_counts=block_counts, hub_rows=hub_rows, w_self=w_self, w_nbr=w_nbr, cotangent=cotangent)


def reference(features, neighbours, send_rows, block_counts, hub_rows, w_self, w_nbr, cotangent):
    node_total = features.shape[0]
    device = (jnp.arange(node_total, dtype=jnp.int32) // NODE_DEV)[:, None]
    group_id = device // N_MEMBER
    member_id = device % N_MEMBER
    local_id = device * NODE_DEV + jnp.clip(neighbours, 0, NODE_DEV - 1)
    shifted = jnp.clip(neighbours - NODE_DEV, 0, N_MEMBER * BLOCK - 1)
    peer = shifted // BLOCK
    slot = shifted % BLOCK
    sender = group_id * N_MEMBER + peer
    pair = sender * N_MEMBER + member_id
    sent = send_rows[pair, slot]
    valid = slot < block_counts[pair]
    border_id = jnp.where(valid, sender * NODE_DEV + sent, node_total)
    hub_pos = jnp.clip(neighbours - NODE_DEV - N_MEMBER * BLOCK, 0, N_GROUP * N_MEMBER * HUB_DEV - 1)
    owner = hub_pos // HUB_DEV
    hub_id = owner * NODE_DEV + hub_rows[owner, hub_pos % HUB_DEV]
    source = jnp.where(neighbours < NODE_DEV, local_id, jnp.where(neighbours < NODE_DEV + N_MEMBER * BLOCK, border_id, hub_id)).astype(jnp.int32)
    extended = jnp.concatenate([features, jnp.zeros((1, D), jnp.bfloat16)], axis=0)
    agg_sum = jnp.zeros((node_total, D), jnp.float32)
    for sample in range(FANOUT):
        agg_sum = agg_sum + extended[source[:, sample]].astype(jnp.float32)
    agg = (agg_sum / FANOUT).astype(jnp.bfloat16)
    pre = jnp.dot(features, w_self, preferred_element_type=jnp.float32) + jnp.dot(agg, w_nbr, preferred_element_type=jnp.float32)
    sigma = jax.nn.sigmoid(pre)
    dpre = (cotangent.astype(jnp.float32) * sigma * (1.0 + pre * (1.0 - sigma))).astype(jnp.bfloat16)
    scale = 1.0 / math.sqrt(node_total)
    grad_self = jnp.dot(features.T, dpre, preferred_element_type=jnp.float32) * scale
    grad_nbr = jnp.dot(agg.T, dpre, preferred_element_type=jnp.float32) * scale
    own_grad = jnp.dot(dpre, w_self.T, preferred_element_type=jnp.float32)
    dagg = jnp.dot(dpre, w_nbr.T, preferred_element_type=jnp.float32) / FANOUT
    spread = jnp.zeros((node_total + 1, D), jnp.float32)
    for sample in range(FANOUT):
        spread = spread.at[source[:, sample]].add(dagg)
    grad_features = (own_grad + spread[:node_total]).astype(jnp.bfloat16)
    return (grad_self, grad_nbr, grad_features)
```

```python
import functools
import math

import jax
import jax.numpy as jnp
from jax import lax
from jax.experimental import pallas as pl
from jax.experimental.pallas import tpu as pltpu
from jax.sharding import PartitionSpec as P

MESH = pl.DeviceIdType.MESH
BF = jnp.bfloat16
F32 = jnp.float32
CHUNK = 256


def dot(a, b):
    return jnp.dot(a, b, preferred_element_type=F32)


def dot_tn(a, b):
    return lax.dot_general(a, b, (((0,), (0,)), ((), ())), preferred_element_type=F32)


def dot_nt(a, b):
    return lax.dot_general(a, b, (((1,), (1,)), ((), ())), preferred_element_type=F32)


def split(value):
    high = value.astype(BF)
    return high, (value - high.astype(F32)).astype(BF)


def wait_bytes(ref, sem):
    pltpu.make_async_copy(ref, ref, sem).wait()


def kernel(
    n_group,
    n_member,
    low,
    block,
    hubs,
    feat_ref,
    nbr_ref,
    sel_ref,
    wself_ref,
    wnbr_ref,
    cot_ref,
    grad_ref,
    total_ref,
    onehot,
    out_border,
    in_border,
    out_hub,
    in_hub,
    back_border,
    ret_border,
    back_hub,
    ret_hub,
    part,
    scattered,
    mine,
    across,
    reduced,
    send_sem,
    recv_sem,
):
    nodes, width = feat_ref.shape
    half = width // 2
    fan = nbr_ref.shape[0]
    owners = n_group * n_member
    hub2 = 2 * hubs
    border_rows = n_member * block
    hub_base = nodes + border_rows
    g = lax.axis_index("group")
    m = lax.axis_index("member")
    me = g * n_member + m
    hi, lo = m // low, m % low
    n_hi = n_member // low
    n_q = n_group * low
    q = g * low + lo
    piece = mine.shape[0]

    barrier = pltpu.get_barrier_semaphore()

    def greet(step, carry):
        peer = (me + step) % owners
        pl.semaphore_signal(
            barrier, inc=1, device_id=(peer // n_member, peer % n_member), device_id_type=MESH
        )
        return carry

    lax.fori_loop(1, owners, greet, 0)

    def copy(src, dst, which, device):
        pltpu.make_async_remote_copy(
            src_ref=src,
            dst_ref=dst,
            send_sem=send_sem.at[which],
            recv_sem=recv_sem.at[which],
            device_id=device,
            device_id_type=MESH,
        ).start()

    def rows(start, count):
        return pl.ds(pl.multiple_of(start * count, count), count)

    def to_members(src, dst, which):
        def body(step, carry):
            peer = (m + step) % n_member
            copy(src.at[rows(peer, block)], dst.at[rows(m, block)], which, (g, peer))
            return carry

        lax.fori_loop(1, n_member, body, 0)

    feat = feat_ref[...]
    slots = border_rows + 128
    row_of = lax.broadcasted_iota(jnp.int32, (nodes, slots), 0)
    pick = jnp.where(row_of == sel_ref[...], 1.0, 0.0).astype(BF)
    picked = dot_tn(pick, feat)
    out_border[...] = picked[:border_rows].astype(BF)
    hub_wide = picked[border_rows : border_rows + hub2]
    lane_row = lax.broadcasted_iota(jnp.int32, (hub2, half), 0)
    out_hub[...] = jnp.where(lane_row < hubs, hub_wide[:, :half], hub_wide[:, half:])

    pl.semaphore_wait(barrier, owners - 1)

    to_members(out_border, in_border, 0)

    def send_hub(step, carry):
        peer = (me + step) % owners
        copy(out_hub, in_hub.at[rows(me, hub2)], 1, (peer // n_member, peer % n_member))
        return carry

    lax.fori_loop(1, owners, send_hub, 0)
    in_border[rows(m, block), :] = out_border[rows(m, block), :]
    in_hub[rows(me, hub2), :] = out_hub[...]

    def count(index, first):
        names = lax.broadcasted_iota(jnp.int32, (CHUNK, nodes), 0) + index * CHUNK
        if first is not None:
            names = first + (names // hub2) * hubs + names % hubs
        total = jnp.zeros((CHUNK, nodes), F32)
        for sample in range(fan):
            total = total + jnp.where(names == nbr_ref[sample : sample + 1, :], 1.0, 0.0)
        return total.astype(BF)

    plain_chunks = hub_base // CHUNK
    hub_chunks = owners * hub2 // CHUNK

    def fill_plain(index, carry):
        onehot[rows(index, CHUNK), :] = count(index, None)
        return carry

    def fill_hub(index, carry):
        onehot[rows(plain_chunks + index, CHUNK), :] = count(index, hub_base)
        return carry

    lax.fori_loop(0, plain_chunks, fill_plain, 0)
    lax.fori_loop(0, hub_chunks, fill_hub, 0)

    pre_self = dot(feat, wself_ref[...])
    agg_sum = dot_tn(onehot[:nodes, :], feat)

    others = (n_member - 1) * block
    wait_bytes(in_border.at[pl.ds(0, others)], recv_sem.at[0])
    agg_sum = agg_sum + dot_tn(onehot[nodes:hub_base, :], in_border[...])
    other_hubs = (owners - 1) * hub2
    wait_bytes(in_hub.at[pl.ds(0, other_hubs)], recv_sem.at[1])
    hub_half = lax.broadcasted_iota(jnp.int32, (owners * hub2, half), 0) % hub2 < hubs
    hub_rows = in_hub[...]
    zero = jnp.zeros((), F32)
    hub_table = jnp.concatenate(
        [jnp.where(hub_half, hub_rows, zero), jnp.where(hub_half, zero, hub_rows)], axis=1
    ).astype(BF)
    agg_sum = agg_sum + dot_tn(onehot[hub_base:, :], hub_table)
    agg = (agg_sum / fan).astype(BF)

    pre = pre_self + dot(agg, wnbr_ref[...])
    sigma = jax.nn.sigmoid(pre)
    dpre = (cot_ref[...].astype(F32) * sigma * (1.0 + pre * (1.0 - sigma))).astype(BF)

    part_self = dot_tn(feat, dpre).astype(BF)
    part_nbr = dot_tn(agg, dpre).astype(BF)
    part[0:width, :] = part_self[:, :half]
    part[width : 2 * width, :] = part_self[:, half:]
    part[2 * width : 3 * width, :] = part_nbr[:, :half]
    part[3 * width :, :] = part_nbr[:, half:]

    def near(step):
        peer = (q + step) % n_q
        return peer, (peer // low, hi * low + peer % low)

    def scatter(step, carry):
        peer, device = near(step)
        copy(part.at[rows(peer, piece)], scattered.at[rows(q, piece)], 2, device)
        return carry

    lax.fori_loop(1, n_q, scatter, 0)
    scattered[rows(q, piece), :] = part[rows(q, piece), :]

    dagg = dot_nt(dpre, wnbr_ref[...]) / fan
    dagg_high, dagg_low = split(dagg)

    def spread(start, stop):
        held = onehot[start:stop, :]
        return dot(held, dagg_high) + dot(held, dagg_low)

    back_border[...] = spread(nodes, hub_base).astype(BF)
    to_members(back_border, ret_border, 3)
    ret_border[rows(m, block), :] = back_border[rows(m, block), :]
    hub_wide = spread(hub_base, hub_base + owners * hub2)
    back_hub[...] = jnp.where(hub_half, hub_wide[:, :half], hub_wide[:, half:])

    def send_back(step, carry):
        peer = (me + step) % owners
        copy(
            back_hub.at[rows(peer, hub2)],
            ret_hub.at[rows(me, hub2)],
            4,
            (peer // n_member, peer % n_member),
        )
        return carry

    lax.fori_loop(1, owners, send_back, 0)
    ret_hub[rows(me, hub2), :] = back_hub[rows(me, hub2), :]

    wait_bytes(scattered.at[pl.ds(0, (n_q - 1) * piece)], recv_sem.at[2])
    summed = jnp.zeros((piece, half), F32)
    for index in range(n_q):
        summed = summed + scattered[index * piece : (index + 1) * piece, :].astype(F32)
    mine[...] = summed.astype(BF)

    def cross(step, carry):
        peer = (hi + step) % n_hi
        copy(mine, across.at[rows(hi, piece)], 5, (g, peer * low + lo))
        return carry

    lax.fori_loop(1, n_hi, cross, 0)
    across[rows(hi, piece), :] = mine[...]

    total = dot_nt(dpre, wself_ref[...]) + spread(0, nodes)

    wait_bytes(across.at[pl.ds(0, (n_hi - 1) * piece)], recv_sem.at[5])

    def add_up(index, carry):
        return carry + across[rows(index, piece), :].astype(F32)

    reduced[...] = lax.fori_loop(0, n_hi, add_up, jnp.zeros((piece, half), F32)).astype(BF)

    def gather(step, carry):
        _, device = near(step)
        copy(reduced, grad_ref.at[rows(q, piece)], 6, device)
        return carry

    lax.fori_loop(1, n_q, gather, 0)
    grad_ref[rows(q, piece), :] = reduced[...]

    wait_bytes(ret_border.at[pl.ds(0, others)], recv_sem.at[3])
    total = total + dot(pick[:, :border_rows], ret_border[...])
    wait_bytes(ret_hub.at[pl.ds(0, other_hubs)], recv_sem.at[4])
    hub_sum = jnp.sum(ret_hub[...].reshape(owners, hub2, half), axis=0)
    top = lane_row < hubs
    hub_sum = jnp.concatenate(
        [jnp.where(top, hub_sum, zero), jnp.where(top, zero, hub_sum)], axis=1
    )
    hub_high, hub_low = split(hub_sum)
    hub_back = jnp.concatenate(
        [
            hub_high.astype(F32),
            hub_low.astype(F32),
            jnp.zeros((128 - 2 * hub2, width), F32),
        ],
        axis=0,
    ).astype(BF)
    total_ref[...] = total + dot(pick[:, border_rows:], hub_back)

    wait_bytes(grad_ref.at[pl.ds(0, (n_q - 1) * piece)], recv_sem.at[6])
    wait_bytes(out_border.at[pl.ds(0, others)], send_sem.at[0])
    wait_bytes(in_hub.at[pl.ds(0, other_hubs)], send_sem.at[1])
    wait_bytes(part.at[pl.ds(0, (n_q - 1) * piece)], send_sem.at[2])
    wait_bytes(back_border.at[pl.ds(0, others)], send_sem.at[3])
    wait_bytes(back_hub.at[pl.ds(0, other_hubs)], send_sem.at[4])
    wait_bytes(across.at[pl.ds(0, (n_hi - 1) * piece)], send_sem.at[5])
    wait_bytes(grad_ref.at[pl.ds(0, (n_q - 1) * piece)], send_sem.at[6])


def local(features, neighbours, send_rows, block_counts, hub_rows, w_self, w_nbr, cotangent):
    nodes, width = features.shape
    n_member = lax.axis_size("member")
    n_group = lax.axis_size("group")
    block = send_rows.shape[1]
    hubs = hub_rows.shape[1]
    owners = n_group * n_member
    hub2 = 2 * hubs
    low = max(1, 8 // n_group)
    piece = 4 * width // (n_group * low)
    half = width // 2
    border_rows = n_member * block
    table_rows = nodes + border_rows + owners * hub2
    keep = jnp.arange(block, dtype=jnp.int32)[None, :] < block_counts[:, None]
    sel = jnp.concatenate(
        [
            jnp.where(keep, send_rows, -1).reshape(1, -1),
            jnp.tile(hub_rows, (1, 4)),
            jnp.full((1, 128 - 4 * hubs), -1, jnp.int32),
        ],
        axis=1,
    )
    vmem = pl.BlockSpec(memory_space=pltpu.VMEM)
    grads, total = pl.pallas_call(
        functools.partial(kernel, n_group, n_member, low, block, hubs),
        out_shape=(
            jax.ShapeDtypeStruct((4 * width, half), BF),
            jax.ShapeDtypeStruct((nodes, width), F32),
        ),
        in_specs=[vmem] * 6,
        out_specs=(vmem, vmem),
        scratch_shapes=[
            pltpu.VMEM((table_rows, nodes), BF),
            pltpu.VMEM((border_rows, width), BF),
            pltpu.VMEM((border_rows, width), BF),
            pltpu.VMEM((hub2, half), F32),
            pltpu.VMEM((owners * hub2, half), F32),
            pltpu.VMEM((border_rows, width), BF),
            pltpu.VMEM((border_rows, width), BF),
            pltpu.VMEM((owners * hub2, half), F32),
            pltpu.VMEM((owners * hub2, half), F32),
            pltpu.VMEM((4 * width, half), BF),
            pltpu.VMEM((4 * width, half), BF),
            pltpu.VMEM((piece, half), BF),
            pltpu.VMEM((n_member // low * piece, half), BF),
            pltpu.VMEM((piece, half), BF),
            pltpu.SemaphoreType.DMA((7,)),
            pltpu.SemaphoreType.DMA((7,)),
        ],
        compiler_params=pltpu.CompilerParams(
            collective_id=0, has_side_effects=True, vmem_limit_bytes=40 * 1024 * 1024
        ),
    )(features, neighbours.T, sel, w_self, w_nbr, cotangent)
    scale = 1.0 / math.sqrt(nodes * owners)
    grads = grads.astype(F32) * scale
    grad_self = jnp.concatenate([grads[:width], grads[width : 2 * width]], axis=1)
    grad_nbr = jnp.concatenate([grads[2 * width : 3 * width], grads[3 * width :]], axis=1)
    return (grad_self, grad_nbr, total.astype(BF))


def solution(mesh):
    in_specs = (
        P(("group", "member"), None),
        P(("group", "member"), None),
        P(("group", "member"), None),
        P(("group", "member")),
        P(("group", "member"), None),
        P(),
        P(),
        P(("group", "member"), None),
    )
    out_specs = (P(), P(), P(("group", "member"), None))
    return jax.shard_map(local, mesh=mesh, in_specs=in_specs, out_specs=out_specs, check_vma=False)
```

```python
import functools
import math

import jax
import jax.numpy as jnp
from jax import lax
from jax.experimental import pallas as pl
from jax.experimental.pallas import tpu as pltpu
from jax.sharding import PartitionSpec as P

MESH = pl.DeviceIdType.MESH
BF = jnp.bfloat16
F32 = jnp.float32
CHUNK = 256


def dot(a, b):
    return jnp.dot(a, b, preferred_element_type=F32)


def dot_tn(a, b):
    return lax.dot_general(a, b, (((0,), (0,)), ((), ())), preferred_element_type=F32)


def dot_nt(a, b):
    return lax.dot_general(a, b, (((1,), (1,)), ((), ())), preferred_element_type=F32)


def split(value):
    high = value.astype(BF)
    return high, (value - high.astype(F32)).astype(BF)


def wait_bytes(ref, sem):
    pltpu.make_async_copy(ref, ref, sem).wait()


def select_rows(n_member, block, send_rows, counts):
    lanes = n_member * block
    lane = lax.broadcasted_iota(jnp.int32, (n_member, lanes), 1)
    peer = lax.broadcasted_iota(jnp.int32, (n_member, lanes), 0)
    own = lane // block == peer
    slot = lax.broadcasted_iota(jnp.int32, (block, lanes), 0)
    slot_lane = lax.broadcasted_iota(jnp.int32, (block, lanes), 1) % block
    expand = jnp.where(slot == slot_lane, 1.0, 0.0).astype(BF)
    spread_rows = dot(send_rows.astype(F32).astype(BF), expand)
    row = jnp.sum(jnp.where(own, spread_rows, 0.0), axis=0, keepdims=True)
    repeat = jnp.where(own, 1.0, 0.0).astype(BF)
    counts = jnp.broadcast_to(counts.astype(F32), (8, n_member)).astype(BF)
    live = dot(counts, repeat)[:1].astype(jnp.int32)
    lane = lax.broadcasted_iota(jnp.int32, (1, lanes), 1)
    return jnp.where(lane % block < live, row.astype(jnp.int32), -1)


def select_hubs(hubs, hub_rows):
    lane = lax.broadcasted_iota(jnp.int32, (hubs, 128), 1)
    hub = lax.broadcasted_iota(jnp.int32, (hubs, 128), 0)
    repeat = jnp.where(lane % hubs == hub, 1.0, 0.0).astype(BF)
    wide = jnp.broadcast_to(hub_rows.astype(F32), (8, hubs)).astype(BF)
    row = dot(wide, repeat)[:1].astype(jnp.int32)
    lane = lax.broadcasted_iota(jnp.int32, (1, 128), 1)
    return jnp.where(lane < 4 * hubs, row, -1)


def kernel(
    n_group,
    n_member,
    low,
    block,
    hubs,
    feat_hbm,
    nbr_hbm,
    rows_hbm,
    counts_hbm,
    hubs_hbm,
    wself_hbm,
    wnbr_hbm,
    cot_hbm,
    grad_ref,
    total_ref,
    feat_ref,
    nbr_ref,
    rows_ref,
    counts_ref,
    hubs_ref,
    wself_ref,
    wnbr_ref,
    cot_ref,
    load_sem,
    onehot,
    onehot_t,
    out_border,
    in_border,
    out_hub,
    in_hub,
    back_border,
    ret_border,
    back_hub,
    ret_hub,
    part,
    scattered,
    mine,
    across,
    reduced,
    send_sem,
    recv_sem,
):
    nodes, width = feat_ref.shape
    half = width // 2
    fan = nbr_ref.shape[0]
    owners = n_group * n_member
    hub2 = 2 * hubs
    border_rows = n_member * block
    hub_base = nodes + border_rows
    g = lax.axis_index("group")
    m = lax.axis_index("member")
    me = g * n_member + m
    hi, lo = m // low, m % low
    n_hi = n_member // low
    n_q = n_group * low
    q = g * low + lo
    piece = mine.shape[0]

    loads = [
        pltpu.make_async_copy(src, dst, load_sem.at[index])
        for index, (src, dst) in enumerate(
            (
                (rows_hbm, rows_ref),
                (counts_hbm, counts_ref),
                (hubs_hbm, hubs_ref),
                (feat_hbm, feat_ref),
                (nbr_hbm, nbr_ref),
                (wself_hbm, wself_ref),
                (wnbr_hbm, wnbr_ref),
                (cot_hbm, cot_ref),
            )
        )
    ]
    for load in loads:
        load.start()

    barrier = pltpu.get_barrier_semaphore()

    def greet(step, carry):
        peer = (me + step) % owners
        pl.semaphore_signal(
            barrier, inc=1, device_id=(peer // n_member, peer % n_member), device_id_type=MESH
        )
        return carry

    lax.fori_loop(1, owners, greet, 0)

    def copy(src, dst, which, device):
        pltpu.make_async_remote_copy(
            src_ref=src,
            dst_ref=dst,
            send_sem=send_sem.at[which],
            recv_sem=recv_sem.at[which],
            device_id=device,
            device_id_type=MESH,
        ).start()

    def rows(start, count):
        return pl.ds(pl.multiple_of(start * count, count), count)

    def to_members(src, dst, which):
        def body(step, carry):
            peer = (m + step) % n_member
            copy(src.at[rows(peer, block)], dst.at[rows(m, block)], which, (g, peer))
            return carry

        lax.fori_loop(1, n_member, body, 0)

    for load in loads[:4]:
        load.wait()
    feat = feat_ref[...]
    sel_rows = select_rows(n_member, block, rows_ref[...], counts_ref[...])
    sel = jnp.concatenate([sel_rows, select_hubs(hubs, hubs_ref[...])], axis=1)
    row_of = lax.broadcasted_iota(jnp.int32, (nodes, border_rows + 128), 0)
    pick = jnp.where(row_of == sel, 1.0, 0.0).astype(BF)
    picked = dot_tn(pick, feat)
    out_border[...] = picked[:border_rows].astype(BF)
    hub_wide = picked[border_rows : border_rows + hub2]
    lane_row = lax.broadcasted_iota(jnp.int32, (hub2, half), 0)
    out_hub[...] = jnp.where(lane_row < hubs, hub_wide[:, :half], hub_wide[:, half:]).astype(BF)

    pl.semaphore_wait(barrier, owners - 1)

    to_members(out_border, in_border, 0)

    def send_hub(step, carry):
        peer = (me + step) % owners
        copy(out_hub, in_hub.at[me], 1, (peer // n_member, peer % n_member))
        return carry

    lax.fori_loop(1, owners, send_hub, 0)
    in_border[rows(m, block), :] = out_border[rows(m, block), :]
    in_hub[me] = out_hub[...]

    for load in loads[4:]:
        load.wait()

    def count(index, first):
        names = lax.broadcasted_iota(jnp.int32, (CHUNK, nodes), 0) + index * CHUNK
        if first is not None:
            names = first + (names // hub2) * hubs + names % hubs
        total = jnp.zeros((CHUNK, nodes), F32)
        for sample in range(fan):
            total = total + jnp.where(names == nbr_ref[sample : sample + 1, :], 1.0, 0.0)
        return total

    plain_chunks = hub_base // CHUNK
    hub_chunks = owners * hub2 // CHUNK

    def fill_plain(index, carry):
        total = count(index, None)
        onehot[rows(index, CHUNK), :] = total.astype(BF)
        onehot_t[:, rows(index, CHUNK)] = total.T.astype(BF)
        return carry

    def fill_hub(index, carry):
        total = count(index, hub_base)
        onehot[rows(plain_chunks + index, CHUNK), :] = total.astype(BF)
        onehot_t[:, rows(plain_chunks + index, CHUNK)] = total.T.astype(BF)
        return carry

    lax.fori_loop(0, plain_chunks, fill_plain, 0)
    lax.fori_loop(0, hub_chunks, fill_hub, 0)

    pre_self = dot(feat, wself_ref[...])
    agg_sum = dot(onehot_t[:, :nodes], feat)
    feat_t = feat.astype(F32).T.astype(BF)

    others = (n_member - 1) * block
    wait_bytes(in_border.at[pl.ds(0, others)], recv_sem.at[0])
    agg_sum = agg_sum + dot(onehot_t[:, nodes:hub_base], in_border[...])
    other_hubs = owners - 1
    wait_bytes(in_hub.at[pl.ds(0, other_hubs)], recv_sem.at[1])
    hub_half = lax.broadcasted_iota(jnp.int32, (owners * hub2, half), 0) % hub2 < hubs
    hub_rows = in_hub[...].astype(F32).reshape(owners * hub2, half)
    zero = jnp.zeros((), F32)
    hub_table = jnp.concatenate(
        [jnp.where(hub_half, hub_rows, zero), jnp.where(hub_half, zero, hub_rows)], axis=1
    ).astype(BF)
    agg_sum = agg_sum + dot(onehot_t[:, hub_base:], hub_table)
    agg = (agg_sum / fan).astype(BF)

    pre = pre_self + dot(agg, wnbr_ref[...])
    sigma = jax.nn.sigmoid(pre)
    dpre = (cot_ref[...].astype(F32) * sigma * (1.0 + pre * (1.0 - sigma))).astype(BF)

    part_self = dot(feat_t, dpre).astype(BF)
    part_nbr = dot_tn(agg, dpre).astype(BF)
    part[0:width, :] = part_self[:, :half]
    part[width : 2 * width, :] = part_self[:, half:]
    part[2 * width : 3 * width, :] = part_nbr[:, :half]
    part[3 * width :, :] = part_nbr[:, half:]

    def near(step):
        peer = (q + step) % n_q
        return peer, (peer // low, hi * low + peer % low)

    def scatter(step, carry):
        peer, device = near(step)
        copy(part.at[rows(peer, piece)], scattered.at[rows(q, piece)], 2, device)
        return carry

    lax.fori_loop(1, n_q, scatter, 0)
    scattered[rows(q, piece), :] = part[rows(q, piece), :]

    dagg = dot_nt(dpre, wnbr_ref[...]) / fan
    dagg_high, dagg_low = split(dagg)

    def spread(start, stop):
        held = onehot[start:stop, :]
        return dot(held, dagg_high) + dot(held, dagg_low)

    back_border[...] = spread(nodes, hub_base).astype(BF)
    to_members(back_border, ret_border, 3)
    ret_border[rows(m, block), :] = back_border[rows(m, block), :]
    hub_wide = spread(hub_base, hub_base + owners * hub2)
    hub_wide = jnp.where(hub_half, hub_wide[:, :half], hub_wide[:, half:])
    back_hub[...] = hub_wide.reshape(owners, hub2, half).astype(BF)

    def send_back(step, carry):
        peer = (me + step) % owners
        copy(
            back_hub.at[peer],
            ret_hub.at[me],
            4,
            (peer // n_member, peer % n_member),
        )
        return carry

    lax.fori_loop(1, owners, send_back, 0)
    ret_hub[me] = back_hub[me]

    wait_bytes(scattered.at[pl.ds(0, (n_q - 1) * piece)], recv_sem.at[2])
    summed = jnp.zeros((piece, half), F32)
    for index in range(n_q):
        summed = summed + scattered[index * piece : (index + 1) * piece, :].astype(F32)
    mine[...] = summed.astype(BF)

    def cross(step, carry):
        peer = (hi + step) % n_hi
        copy(mine, across.at[rows(hi, piece)], 5, (g, peer * low + lo))
        return carry

    lax.fori_loop(1, n_hi, cross, 0)
    across[rows(hi, piece), :] = mine[...]

    total = dot_nt(dpre, wself_ref[...]) + spread(0, nodes)

    wait_bytes(across.at[pl.ds(0, (n_hi - 1) * piece)], recv_sem.at[5])

    def add_up(index, carry):
        return carry + across[rows(index, piece), :].astype(F32)

    reduced[...] = lax.fori_loop(0, n_hi, add_up, jnp.zeros((piece, half), F32)).astype(BF)

    def gather(step, carry):
        _, device = near(step)
        copy(reduced, grad_ref.at[rows(q, piece)], 6, device)
        return carry

    lax.fori_loop(1, n_q, gather, 0)
    grad_ref[rows(q, piece), :] = reduced[...]

    wait_bytes(ret_border.at[pl.ds(0, others)], recv_sem.at[3])
    total = total + dot(pick[:, :border_rows], ret_border[...])
    wait_bytes(ret_hub.at[pl.ds(0, other_hubs)], recv_sem.at[4])
    hub_sum = jnp.sum(ret_hub[...].astype(F32), axis=0)
    top = lane_row < hubs
    hub_sum = jnp.concatenate(
        [jnp.where(top, hub_sum, zero), jnp.where(top, zero, hub_sum)], axis=1
    )
    hub_high, hub_low = split(hub_sum)
    hub_back = jnp.concatenate(
        [
            hub_high.astype(F32),
            hub_low.astype(F32),
            jnp.zeros((128 - 2 * hub2, width), F32),
        ],
        axis=0,
    ).astype(BF)
    total_ref[...] = total + dot(pick[:, border_rows:], hub_back)

    wait_bytes(grad_ref.at[pl.ds(0, (n_q - 1) * piece)], recv_sem.at[6])
    wait_bytes(out_border.at[pl.ds(0, others)], send_sem.at[0])
    wait_bytes(in_hub.at[pl.ds(0, other_hubs)], send_sem.at[1])
    wait_bytes(part.at[pl.ds(0, (n_q - 1) * piece)], send_sem.at[2])
    wait_bytes(back_border.at[pl.ds(0, others)], send_sem.at[3])
    wait_bytes(back_hub.at[pl.ds(0, other_hubs)], send_sem.at[4])
    wait_bytes(across.at[pl.ds(0, (n_hi - 1) * piece)], send_sem.at[5])
    wait_bytes(grad_ref.at[pl.ds(0, (n_q - 1) * piece)], send_sem.at[6])


def local(features, neighbours, send_rows, block_counts, hub_rows, w_self, w_nbr, cotangent):
    nodes, width = features.shape
    n_member = lax.axis_size("member")
    n_group = lax.axis_size("group")
    block = send_rows.shape[1]
    hubs = hub_rows.shape[1]
    owners = n_group * n_member
    hub2 = 2 * hubs
    low = max(1, 8 // n_group)
    piece = 4 * width // (n_group * low)
    half = width // 2
    border_rows = n_member * block
    table_rows = nodes + border_rows + owners * hub2
    vmem = pl.BlockSpec(memory_space=pltpu.VMEM)
    grads, total = pl.pallas_call(
        functools.partial(kernel, n_group, n_member, low, block, hubs),
        out_shape=(
            pltpu.VMEM((4 * width, half), BF),
            pltpu.VMEM((nodes, width), F32),
        ),
        in_specs=[pl.BlockSpec(memory_space=pltpu.HBM)] * 8,
        out_specs=(vmem, vmem),
        scratch_shapes=[
            pltpu.VMEM((nodes, width), BF),
            pltpu.VMEM((neighbours.shape[1], nodes), jnp.int32),
            pltpu.VMEM(send_rows.shape, jnp.int32),
            pltpu.VMEM((1, n_member), jnp.int32),
            pltpu.VMEM(hub_rows.shape, jnp.int32),
            pltpu.VMEM((width, width), BF),
            pltpu.VMEM((width, width), BF),
            pltpu.VMEM((nodes, width), BF),
            pltpu.SemaphoreType.DMA((8,)),
            pltpu.VMEM((table_rows, nodes), BF),
            pltpu.VMEM((nodes, table_rows), BF),
            pltpu.VMEM((border_rows, width), BF),
            pltpu.VMEM((border_rows, width), BF),
            pltpu.VMEM((hub2, half), BF),
            pltpu.VMEM((owners, hub2, half), BF),
            pltpu.VMEM((border_rows, width), BF),
            pltpu.VMEM((border_rows, width), BF),
            pltpu.VMEM((owners, hub2, half), BF),
            pltpu.VMEM((owners, hub2, half), BF),
            pltpu.VMEM((4 * width, half), BF),
            pltpu.VMEM((4 * width, half), BF),
            pltpu.VMEM((piece, half), BF),
            pltpu.VMEM((n_member // low * piece, half), BF),
            pltpu.VMEM((piece, half), BF),
            pltpu.SemaphoreType.DMA((7,)),
            pltpu.SemaphoreType.DMA((7,)),
        ],
        compiler_params=pltpu.CompilerParams(
            collective_id=0, has_side_effects=True, vmem_limit_bytes=60 * 1024 * 1024
        ),
    )(
        features,
        neighbours.T,
        send_rows,
        block_counts.reshape(1, -1),
        hub_rows,
        w_self,
        w_nbr,
        cotangent,
    )
    scale = 1.0 / math.sqrt(nodes * owners)
    grads = grads.astype(F32) * scale
    grad_self = jnp.concatenate([grads[:width], grads[width : 2 * width]], axis=1)
    grad_nbr = jnp.concatenate([grads[2 * width : 3 * width], grads[3 * width :]], axis=1)
    return (grad_self, grad_nbr, total.astype(BF))


def solution(mesh):
    in_specs = (
        P(("group", "member"), None),
        P(("group", "member"), None),
        P(("group", "member"), None),
        P(("group", "member")),
        P(("group", "member"), None),
        P(),
        P(),
        P(("group", "member"), None),
    )
    out_specs = (P(), P(), P(("group", "member"), None))
    return jax.shard_map(local, mesh=mesh, in_specs=in_specs, out_specs=out_specs, check_vma=False)
```

```python
import functools
import math

import jax
import jax.numpy as jnp
from jax import lax
from jax.experimental import pallas as pl
from jax.experimental.pallas import tpu as pltpu
from jax.sharding import PartitionSpec as P

MESH = pl.DeviceIdType.MESH
BF = jnp.bfloat16
F32 = jnp.float32
CHUNK = 256


def dot(a, b):
    return jnp.dot(a, b, preferred_element_type=F32)


def dot_tn(a, b):
    return lax.dot_general(a, b, (((0,), (0,)), ((), ())), preferred_element_type=F32)


def dot_nt(a, b):
    return lax.dot_general(a, b, (((1,), (1,)), ((), ())), preferred_element_type=F32)


def split(value):
    high = value.astype(BF)
    return high, (value - high.astype(F32)).astype(BF)


def wait_bytes(ref, sem):
    pltpu.make_async_copy(ref, ref, sem).wait()


def select_rows(n_member, block, send_rows, counts):
    lanes = n_member * block
    lane = lax.broadcasted_iota(jnp.int32, (n_member, lanes), 1)
    peer = lax.broadcasted_iota(jnp.int32, (n_member, lanes), 0)
    own = lane // block == peer
    slot = lax.broadcasted_iota(jnp.int32, (block, lanes), 0)
    slot_lane = lax.broadcasted_iota(jnp.int32, (block, lanes), 1) % block
    expand = jnp.where(slot == slot_lane, 1.0, 0.0).astype(BF)
    spread_rows = dot(send_rows.astype(F32).astype(BF), expand)
    row = jnp.sum(jnp.where(own, spread_rows, 0.0), axis=0, keepdims=True)
    repeat = jnp.where(own, 1.0, 0.0).astype(BF)
    counts = jnp.broadcast_to(counts.astype(F32), (8, n_member)).astype(BF)
    live = dot(counts, repeat)[:1].astype(jnp.int32)
    lane = lax.broadcasted_iota(jnp.int32, (1, lanes), 1)
    return jnp.where(lane % block < live, row.astype(jnp.int32), -1)


def select_hubs(hubs, hub_rows):
    lane = lax.broadcasted_iota(jnp.int32, (hubs, 128), 1)
    hub = lax.broadcasted_iota(jnp.int32, (hubs, 128), 0)
    repeat = jnp.where(lane % hubs == hub, 1.0, 0.0).astype(BF)
    wide = jnp.broadcast_to(hub_rows.astype(F32), (8, hubs)).astype(BF)
    row = dot(wide, repeat)[:1].astype(jnp.int32)
    lane = lax.broadcasted_iota(jnp.int32, (1, 128), 1)
    return jnp.where(lane < 4 * hubs, row, -1)


def kernel(
    n_group,
    n_member,
    low,
    block,
    hubs,
    feat_hbm,
    nbr_hbm,
    rows_hbm,
    counts_hbm,
    hubs_hbm,
    wself_hbm,
    wnbr_hbm,
    cot_hbm,
    out_ref,
    feat_ref,
    nbr_ref,
    rows_ref,
    counts_ref,
    hubs_ref,
    wself_ref,
    wnbr_ref,
    cot_ref,
    load_sem,
    onehot,
    onehot_t,
    out_border,
    in_border,
    out_hub,
    line_hub,
    in_hub,
    back_border,
    ret_border,
    back_hub,
    ret_hub,
    line_back,
    line_ret,
    part,
    scattered,
    mine,
    across,
    reduced,
    send_sem,
    recv_sem,
):
    nodes, width = feat_ref.shape
    half = width // 2
    fan = nbr_ref.shape[0]
    owners = n_group * n_member
    hub2 = 2 * hubs
    border_rows = n_member * block
    hub_base = nodes + border_rows
    g = lax.axis_index("group")
    m = lax.axis_index("member")
    hi, lo = lax.div(m, low), lax.rem(m, low)
    n_hi = n_member // low
    n_q = n_group * low
    q = g * low + lo
    piece = width // n_q

    loads = [
        pltpu.make_async_copy(src, dst, load_sem.at[index])
        for index, (src, dst) in enumerate(
            (
                (rows_hbm, rows_ref),
                (counts_hbm, counts_ref),
                (hubs_hbm, hubs_ref),
                (feat_hbm, feat_ref),
                (nbr_hbm, nbr_ref),
                (wself_hbm, wself_ref),
                (wnbr_hbm, wnbr_ref),
                (cot_hbm, cot_ref),
            )
        )
    ]
    for load in loads:
        load.start()

    def loop(count, body):
        lax.fori_loop(1, count, lambda step, carry: (body(step), carry)[1], 0, unroll=count <= 16)

    def member(step):
        peer = lax.rem(m + step, n_member)
        return peer, (g, peer)

    def near(step):
        peer = lax.rem(q + step, n_q)
        return peer, (lax.div(peer, low), hi * low + lax.rem(peer, low))

    def line(step):
        peer = lax.rem(hi + step, n_hi)
        return peer, (g, peer * low + lo)

    barrier = pltpu.get_barrier_semaphore()

    def greet(device):
        pl.semaphore_signal(barrier, inc=1, device_id=device, device_id_type=MESH)

    loop(n_member, lambda step: greet(member(step)[1]))
    for step in range(1, n_group):
        for other in range(low):
            greet((lax.rem(g + step, n_group), hi * low + other))

    def copy(src, dst, which, device):
        pltpu.make_async_remote_copy(
            src_ref=src,
            dst_ref=dst,
            send_sem=send_sem.at[which],
            recv_sem=recv_sem.at[which],
            device_id=device,
            device_id_type=MESH,
        ).start()

    def rows(start, count):
        return pl.ds(pl.multiple_of(start * count, count), count)

    def to_members(src, dst, which):
        def body(step):
            peer, device = member(step)
            copy(src.at[rows(peer, block)], dst.at[rows(m, block)], which, device)

        loop(n_member, body)
        dst[rows(m, block), :] = src[rows(m, block), :]

    for load in loads[:4]:
        load.wait()
    feat = feat_ref[...]
    sel_rows = select_rows(n_member, block, rows_ref[...], counts_ref[...])
    sel = jnp.concatenate([sel_rows, select_hubs(hubs, hubs_ref[...])], axis=1)
    row_of = lax.broadcasted_iota(jnp.int32, (nodes, border_rows + 128), 0)
    pick = jnp.where(row_of == sel, 1.0, 0.0).astype(BF)
    picked = dot_tn(pick, feat)
    out_border[...] = picked[:border_rows].astype(BF)
    hub_wide = picked[border_rows : border_rows + hub2]
    lane_row = lax.broadcasted_iota(jnp.int32, (hub2, half), 0)
    out_hub[...] = jnp.where(lane_row < hubs, hub_wide[:, :half], hub_wide[:, half:]).astype(BF)

    pl.semaphore_wait(barrier, n_member - 1 + (n_group - 1) * low)

    loop(n_hi, lambda step: copy(out_hub, line_hub.at[hi], 1, line(step)[1]))
    line_hub[hi] = out_hub[...]
    to_members(out_border, in_border, 0)

    for load in loads[4:]:
        load.wait()

    def count(names):
        names = jnp.concatenate([names] * (nodes // 128), axis=1)
        total = jnp.zeros((CHUNK, nodes), F32)
        for sample in range(fan):
            total = total + jnp.where(names == nbr_ref[sample : sample + 1, :], 1.0, 0.0)
        return total

    def chunk_names(index):
        return lax.broadcasted_iota(jnp.int32, (CHUNK, 128), 0) + index * CHUNK

    def store(index, total):
        onehot[rows(index, CHUNK), :] = total.astype(BF)
        onehot_t[:, rows(index, CHUNK)] = total.T.astype(BF)

    plain_chunks = hub_base // CHUNK
    hub_chunks = owners * hub2 // CHUNK

    def fill_plain(index, carry):
        store(index, count(chunk_names(index)))
        return carry

    def fill_hub(index, carry):
        row = chunk_names(index)
        slab = lax.div(row, hub2)
        near_id = lax.div(slab, n_hi)
        owner = (
            lax.div(near_id, low) * n_member + lax.rem(slab, n_hi) * low + lax.rem(near_id, low)
        )
        store(plain_chunks + index, count(hub_base + owner * hubs + lax.rem(row, hubs)))
        return carry

    lax.fori_loop(0, plain_chunks, fill_plain, 0)

    wait_bytes(line_hub.at[pl.ds(0, n_hi - 1)], recv_sem.at[1])
    loop(n_q, lambda step: copy(line_hub, in_hub.at[q], 2, near(step)[1]))
    in_hub[q] = line_hub[...]

    lax.fori_loop(0, hub_chunks, fill_hub, 0)
    pre_self = dot(feat, wself_ref[...])
    agg_sum = dot(onehot_t[:, :nodes], feat)
    feat_t = feat.astype(F32).T.astype(BF)

    others = (n_member - 1) * block
    wait_bytes(in_border.at[pl.ds(0, others)], recv_sem.at[0])
    agg_sum = agg_sum + dot(onehot_t[:, nodes:hub_base], in_border[...])
    wait_bytes(in_hub.at[pl.ds(0, n_q - 1)], recv_sem.at[2])
    hub_half = lax.broadcasted_iota(jnp.int32, (owners * hub2, half), 0) % hub2 < hubs
    hub_rows = in_hub[...].astype(F32).reshape(owners * hub2, half)
    zero = jnp.zeros((), F32)
    hub_table = jnp.concatenate(
        [jnp.where(hub_half, hub_rows, zero), jnp.where(hub_half, zero, hub_rows)], axis=1
    ).astype(BF)
    agg_sum = agg_sum + dot(onehot_t[:, hub_base:], hub_table)
    agg = (agg_sum / fan).astype(BF)

    pre = pre_self + dot(agg, wnbr_ref[...])
    sigma = jax.nn.sigmoid(pre)
    dpre = (cot_ref[...].astype(F32) * sigma * (1.0 + pre * (1.0 - sigma))).astype(BF)

    def scatter(which):
        def body(step):
            peer, device = near(step)
            copy(
                part.at[rows(which * n_q + peer, piece)],
                scattered.at[rows(which * n_q + q, piece)],
                3 + which,
                device,
            )

        loop(n_q, body)
        own = rows(which * n_q + q, piece)
        scattered[own, :] = part[own, :]

    part[:width, :] = dot(feat_t, dpre).astype(BF)
    scatter(0)
    part[width:, :] = dot_tn(agg, dpre).astype(BF)
    scatter(1)

    dagg = dot_nt(dpre, wnbr_ref[...]) / fan
    dagg_high, dagg_low = split(dagg)

    def spread(start, stop):
        held = onehot[start:stop, :]
        return dot(held, dagg_high) + dot(held, dagg_low)

    hub_wide = spread(hub_base, hub_base + owners * hub2)
    hub_wide = jnp.where(hub_half, hub_wide[:, :half], hub_wide[:, half:])
    back_hub[...] = hub_wide.reshape(n_q, n_hi, hub2, half).astype(BF)

    def send_back(step):
        peer, device = near(step)
        copy(back_hub.at[peer], ret_hub.at[q], 10, device)

    loop(n_q, send_back)
    ret_hub[q] = back_hub[q]
    back_border[...] = spread(nodes, hub_base).astype(BF)
    to_members(back_border, ret_border, 9)

    near_rows = (n_q - 1) * piece
    line_rows = (n_hi - 1) * piece

    def cross(which):
        wait_bytes(scattered.at[pl.ds(which * width, near_rows)], recv_sem.at[3 + which])
        summed = jnp.zeros((piece, width), F32)
        for index in range(n_q):
            start = which * width + index * piece
            summed = summed + scattered[start : start + piece, :].astype(F32)
        source = mine.at[pl.ds(which * piece, piece)]
        source[...] = summed.astype(BF)
        slot = rows(which * n_hi + hi, piece)
        loop(n_hi, lambda step: copy(source, across.at[slot], 5 + which, line(step)[1]))
        across[slot, :] = source[...]

    cross(0)
    cross(1)

    total = dot_nt(dpre, wself_ref[...]) + spread(0, nodes)

    wait_bytes(ret_hub.at[pl.ds(0, n_q - 1)], recv_sem.at[10])
    line_back[...] = jnp.sum(ret_hub[...].astype(F32), axis=0).astype(BF)

    def send_line(step):
        peer, device = line(step)
        copy(line_back.at[peer], line_ret.at[hi], 11, device)

    loop(n_hi, send_line)
    line_ret[hi] = line_back[hi]

    def gather(which):
        first = which * n_hi
        wait_bytes(across.at[pl.ds(first * piece, line_rows)], recv_sem.at[5 + which])
        summed = lax.fori_loop(
            0,
            n_hi,
            lambda index, carry: carry + across[rows(first + index, piece), :].astype(F32),
            jnp.zeros((piece, width), F32),
            unroll=n_hi <= 16,
        )
        source = reduced.at[pl.ds(which * piece, piece)]
        source[...] = summed.astype(BF)
        slot = rows(which * n_q + q, piece)
        loop(n_q, lambda step: copy(source, out_ref.at[slot], 7 + which, near(step)[1]))
        out_ref[slot, :] = source[...]

    gather(0)
    gather(1)

    wait_bytes(ret_border.at[pl.ds(0, others)], recv_sem.at[9])
    total = total + dot(pick[:, :border_rows], ret_border[...])
    wait_bytes(line_ret.at[pl.ds(0, n_hi - 1)], recv_sem.at[11])
    hub_sum = jnp.sum(line_ret[...].astype(F32), axis=0)
    top = lane_row < hubs
    hub_sum = jnp.concatenate(
        [jnp.where(top, hub_sum, zero), jnp.where(top, zero, hub_sum)], axis=1
    )
    hub_high, hub_low = split(hub_sum)
    hub_back = jnp.concatenate(
        [
            hub_high.astype(F32),
            hub_low.astype(F32),
            jnp.zeros((128 - 2 * hub2, width), F32),
        ],
        axis=0,
    ).astype(BF)
    out_ref[2 * width :, :] = (total + dot(pick[:, border_rows:], hub_back)).astype(BF)

    wait_bytes(out_border.at[pl.ds(0, others)], send_sem.at[0])
    wait_bytes(line_hub.at[pl.ds(0, n_hi - 1)], send_sem.at[1])
    wait_bytes(in_hub.at[pl.ds(0, n_q - 1)], send_sem.at[2])
    wait_bytes(back_border.at[pl.ds(0, others)], send_sem.at[9])
    wait_bytes(back_hub.at[pl.ds(0, n_q - 1)], send_sem.at[10])
    wait_bytes(line_back.at[pl.ds(0, n_hi - 1)], send_sem.at[11])
    for which in range(2):
        wait_bytes(part.at[pl.ds(which * width, near_rows)], send_sem.at[3 + which])
        wait_bytes(across.at[pl.ds(which * n_hi * piece, line_rows)], send_sem.at[5 + which])
    for which in range(2):
        wait_bytes(out_ref.at[pl.ds(which * width, near_rows)], recv_sem.at[7 + which])
        wait_bytes(part.at[pl.ds(which * width, near_rows)], send_sem.at[7 + which])


def local(features, neighbours, send_rows, block_counts, hub_rows, w_self, w_nbr, cotangent):
    nodes, width = features.shape
    n_member = lax.axis_size("member")
    n_group = lax.axis_size("group")
    block = send_rows.shape[1]
    hubs = hub_rows.shape[1]
    owners = n_group * n_member
    hub2 = 2 * hubs
    low = max(1, 8 // n_group)
    n_q = n_group * low
    n_hi = n_member // low
    piece = width // n_q
    half = width // 2
    border_rows = n_member * block
    table_rows = nodes + border_rows + owners * hub2
    border = pltpu.VMEM((border_rows, width), BF)
    hub_line = pltpu.VMEM((n_hi, hub2, half), BF)
    hub_all = pltpu.VMEM((n_q, n_hi, hub2, half), BF)
    pair = pltpu.VMEM((2 * width, width), BF)
    result = pl.pallas_call(
        functools.partial(kernel, n_group, n_member, low, block, hubs),
        out_shape=pltpu.VMEM((2 * width + nodes, width), BF),
        in_specs=[pl.BlockSpec(memory_space=pltpu.HBM)] * 8,
        out_specs=pl.BlockSpec(memory_space=pltpu.VMEM),
        scratch_shapes=[
            pltpu.VMEM((nodes, width), BF),
            pltpu.VMEM((neighbours.shape[1], nodes), jnp.int32),
            pltpu.VMEM(send_rows.shape, jnp.int32),
            pltpu.VMEM((1, n_member), jnp.int32),
            pltpu.VMEM(hub_rows.shape, jnp.int32),
            pltpu.VMEM((width, width), BF),
            pltpu.VMEM((width, width), BF),
            pltpu.VMEM((nodes, width), BF),
            pltpu.SemaphoreType.DMA((8,)),
            pltpu.VMEM((table_rows, nodes), BF),
            pltpu.VMEM((nodes, table_rows), BF),
            border,
            border,
            pltpu.VMEM((hub2, half), BF),
            hub_line,
            hub_all,
            border,
            border,
            hub_all,
            hub_all,
            hub_line,
            hub_line,
            pair,
            pair,
            pltpu.VMEM((2 * piece, width), BF),
            pltpu.VMEM((2 * n_hi * piece, width), BF),
            pltpu.VMEM((2 * piece, width), BF),
            pltpu.SemaphoreType.DMA((12,)),
            pltpu.SemaphoreType.DMA((12,)),
        ],
        compiler_params=pltpu.CompilerParams(
            collective_id=0, has_side_effects=True, vmem_limit_bytes=60 * 1024 * 1024
        ),
    )(
        features,
        neighbours.T,
        send_rows,
        block_counts.reshape(1, -1),
        hub_rows,
        w_self,
        w_nbr,
        cotangent,
    )
    scale = 1.0 / math.sqrt(nodes * owners)
    grad_self = result[:width].astype(F32) * scale
    grad_nbr = result[width : 2 * width].astype(F32) * scale
    return (grad_self, grad_nbr, result[2 * width :])


def solution(mesh):
    in_specs = (
        P(("group", "member"), None),
        P(("group", "member"), None),
        P(("group", "member"), None),
        P(("group", "member")),
        P(("group", "member"), None),
        P(),
        P(),
        P(("group", "member"), None),
    )
    out_specs = (P(), P(), P(("group", "member"), None))
    return jax.shard_map(local, mesh=mesh, in_specs=in_specs, out_specs=out_specs, check_vma=False)
```

```python
import functools
import math

import jax
import jax.numpy as jnp
from jax import lax
from jax.experimental import pallas as pl
from jax.experimental.pallas import tpu as pltpu
from jax.sharding import PartitionSpec as P

MESH = pl.DeviceIdType.MESH
BF = jnp.bfloat16
F32 = jnp.float32
CHUNK = 256
CUTS = 4
BORDER, HUB_LINE, HUB_NEAR, BACK_BORDER, BACK_NEAR, BACK_LINE = range(6)
SCATTER, CROSS, GATHER = 6, 6 + CUTS, 6 + 2 * CUTS
SEMS = 6 + 3 * CUTS


def dot(a, b):
    return jnp.dot(a, b, preferred_element_type=F32)


def dot_tn(a, b):
    return lax.dot_general(a, b, (((0,), (0,)), ((), ())), preferred_element_type=F32)


def dot_nt(a, b):
    return lax.dot_general(a, b, (((1,), (1,)), ((), ())), preferred_element_type=F32)


def split(value):
    high = value.astype(BF)
    return high, (value - high.astype(F32)).astype(BF)


def wait_bytes(ref, sem):
    pltpu.make_async_copy(ref, ref, sem).wait()


def select_rows(n_member, block, send_rows, counts):
    lanes = n_member * block
    lane = lax.broadcasted_iota(jnp.int32, (n_member, lanes), 1)
    peer = lax.broadcasted_iota(jnp.int32, (n_member, lanes), 0)
    own = lane // block == peer
    slot = lax.broadcasted_iota(jnp.int32, (block, lanes), 0)
    slot_lane = lax.broadcasted_iota(jnp.int32, (block, lanes), 1) % block
    expand = jnp.where(slot == slot_lane, 1.0, 0.0).astype(BF)
    spread_rows = dot(send_rows.astype(F32).astype(BF), expand)
    row = jnp.sum(jnp.where(own, spread_rows, 0.0), axis=0, keepdims=True)
    repeat = jnp.where(own, 1.0, 0.0).astype(BF)
    counts = jnp.broadcast_to(counts.astype(F32), (8, n_member)).astype(BF)
    live = dot(counts, repeat)[:1].astype(jnp.int32)
    lane = lax.broadcasted_iota(jnp.int32, (1, lanes), 1)
    return jnp.where(lane % block < live, row.astype(jnp.int32), -1)


def select_hubs(hubs, hub_rows):
    lane = lax.broadcasted_iota(jnp.int32, (hubs, 128), 1)
    hub = lax.broadcasted_iota(jnp.int32, (hubs, 128), 0)
    repeat = jnp.where(lane % hubs == hub, 1.0, 0.0).astype(BF)
    wide = jnp.broadcast_to(hub_rows.astype(F32), (8, hubs)).astype(BF)
    row = dot(wide, repeat)[:1].astype(jnp.int32)
    lane = lax.broadcasted_iota(jnp.int32, (1, 128), 1)
    return jnp.where(lane < 4 * hubs, row, -1)


def kernel(
    n_group,
    n_member,
    low,
    block,
    hubs,
    feat_hbm,
    nbr_hbm,
    rows_hbm,
    counts_hbm,
    hubs_hbm,
    wself_hbm,
    wnbr_hbm,
    cot_hbm,
    out_ref,
    feat_ref,
    nbr_ref,
    rows_ref,
    counts_ref,
    hubs_ref,
    wself_ref,
    wnbr_ref,
    cot_ref,
    load_sem,
    onehot,
    onehot_t,
    out_border,
    in_border,
    out_hub,
    line_hub,
    in_hub,
    back_border,
    ret_border,
    back_hub,
    ret_hub,
    line_back,
    line_ret,
    part,
    scattered,
    mine,
    across,
    reduced,
    send_sem,
    recv_sem,
):
    nodes, width = feat_ref.shape
    half = width // 2
    fan = nbr_ref.shape[0]
    owners = n_group * n_member
    hub2 = 2 * hubs
    border_rows = n_member * block
    hub_base = nodes + border_rows
    g = lax.axis_index("group")
    m = lax.axis_index("member")
    hi, lo = lax.div(m, low), lax.rem(m, low)
    n_hi = n_member // low
    n_q = n_group * low
    q = g * low + lo
    piece = 2 * width // (CUTS * n_q)
    cut = n_q * piece

    loads = [
        pltpu.make_async_copy(src, dst, load_sem.at[index])
        for index, (src, dst) in enumerate(
            (
                (rows_hbm, rows_ref),
                (counts_hbm, counts_ref),
                (hubs_hbm, hubs_ref),
                (feat_hbm, feat_ref),
                (nbr_hbm, nbr_ref),
                (wself_hbm, wself_ref),
                (wnbr_hbm, wnbr_ref),
                (cot_hbm, cot_ref),
            )
        )
    ]
    for load in loads:
        load.start()

    def loop(count, body):
        lax.fori_loop(1, count, lambda step, carry: (body(step), carry)[1], 0, unroll=count <= 16)

    def member(step):
        peer = lax.rem(m + step, n_member)
        return peer, (g, peer)

    def near(step):
        peer = lax.rem(q + step, n_q)
        return peer, (lax.div(peer, low), hi * low + lax.rem(peer, low))

    def line(step):
        peer = lax.rem(hi + step, n_hi)
        return peer, (g, peer * low + lo)

    barrier = pltpu.get_barrier_semaphore()

    def greet(device):
        pl.semaphore_signal(barrier, inc=1, device_id=device, device_id_type=MESH)

    loop(n_member, lambda step: greet(member(step)[1]))
    for step in range(1, n_group):
        for other in range(low):
            greet((lax.rem(g + step, n_group), hi * low + other))

    def copy(src, dst, which, device):
        pltpu.make_async_remote_copy(
            src_ref=src,
            dst_ref=dst,
            send_sem=send_sem.at[which],
            recv_sem=recv_sem.at[which],
            device_id=device,
            device_id_type=MESH,
        ).start()

    def rows(start, count):
        return pl.ds(pl.multiple_of(start * count, count), count)

    def to_members(src, dst, which):
        def body(step):
            peer, device = member(step)
            copy(src.at[rows(peer, block)], dst.at[rows(m, block)], which, device)

        loop(n_member, body)
        dst[rows(m, block), :] = src[rows(m, block), :]

    for load in loads[:3]:
        load.wait()
    sel_rows = select_rows(n_member, block, rows_ref[...], counts_ref[...])
    sel = jnp.concatenate([sel_rows, select_hubs(hubs, hubs_ref[...])], axis=1)
    row_of = lax.broadcasted_iota(jnp.int32, (nodes, border_rows + 128), 0)
    pick = jnp.where(row_of == sel, 1.0, 0.0).astype(BF)
    loads[3].wait()
    feat = feat_ref[...]
    picked = dot_tn(pick, feat)
    out_border[...] = picked[:border_rows].astype(BF)
    hub_wide = picked[border_rows : border_rows + hub2]
    lane_row = lax.broadcasted_iota(jnp.int32, (hub2, half), 0)
    out_hub[...] = jnp.where(lane_row < hubs, hub_wide[:, :half], hub_wide[:, half:]).astype(BF)

    pl.semaphore_wait(barrier, n_member - 1 + (n_group - 1) * low)

    loop(n_hi, lambda step: copy(out_hub, line_hub.at[hi], HUB_LINE, line(step)[1]))
    line_hub[hi] = out_hub[...]
    to_members(out_border, in_border, BORDER)

    for load in loads[4:]:
        load.wait()

    def count(names):
        names = jnp.concatenate([names] * (nodes // 128), axis=1)
        total = jnp.zeros((CHUNK, nodes), F32)
        for sample in range(fan):
            total = total + jnp.where(names == nbr_ref[sample : sample + 1, :], 1.0, 0.0)
        return total

    def chunk_names(index):
        return lax.broadcasted_iota(jnp.int32, (CHUNK, 128), 0) + index * CHUNK

    def store(index, total):
        onehot[rows(index, CHUNK), :] = total.astype(BF)
        onehot_t[:, rows(index, CHUNK)] = total.T.astype(BF)

    plain_chunks = hub_base // CHUNK
    hub_chunks = owners * hub2 // CHUNK

    def fill_plain(index, carry):
        store(index, count(chunk_names(index)))
        return carry

    def fill_hub(index, carry):
        row = chunk_names(index)
        slab = lax.div(row, hub2)
        near_id = lax.div(slab, n_hi)
        owner = (
            lax.div(near_id, low) * n_member + lax.rem(slab, n_hi) * low + lax.rem(near_id, low)
        )
        store(plain_chunks + index, count(hub_base + owner * hubs + lax.rem(row, hubs)))
        return carry

    fill_plain(0, 0)

    wait_bytes(line_hub.at[pl.ds(0, n_hi - 1)], recv_sem.at[HUB_LINE])
    loop(n_q, lambda step: copy(line_hub, in_hub.at[q], HUB_NEAR, near(step)[1]))
    in_hub[q] = line_hub[...]

    lax.fori_loop(1, plain_chunks, fill_plain, 0)
    lax.fori_loop(0, hub_chunks, fill_hub, 0)
    pre_self = dot(feat, wself_ref[...])
    agg_sum = dot(onehot_t[:, :nodes], feat)
    feat_t = feat.astype(F32).T.astype(BF)

    wait_bytes(in_hub.at[pl.ds(0, n_q - 1)], recv_sem.at[HUB_NEAR])
    hub_half = lax.broadcasted_iota(jnp.int32, (owners * hub2, half), 0) % hub2 < hubs
    hub_rows = in_hub[...].astype(F32).reshape(owners * hub2, half)
    zero = jnp.zeros((), F32)
    hub_table = jnp.concatenate(
        [jnp.where(hub_half, hub_rows, zero), jnp.where(hub_half, zero, hub_rows)], axis=1
    ).astype(BF)
    agg_sum = agg_sum + dot(onehot_t[:, hub_base:], hub_table)
    others = (n_member - 1) * block
    wait_bytes(in_border.at[pl.ds(0, others)], recv_sem.at[BORDER])
    agg_sum = agg_sum + dot(onehot_t[:, nodes:hub_base], in_border[...])
    agg = (agg_sum * (1.0 / fan)).astype(BF)

    pre = pre_self + dot(agg, wnbr_ref[...])
    sigma = 0.5 * jnp.tanh(0.5 * pre) + 0.5
    dpre = (cot_ref[...].astype(F32) * sigma * (1.0 + pre * (1.0 - sigma))).astype(BF)

    def scatter(which):
        def body(step):
            peer, device = near(step)
            copy(
                part.at[rows(which * n_q + peer, piece)],
                scattered.at[rows(which * n_q + q, piece)],
                SCATTER + which,
                device,
            )

        loop(n_q, body)
        own = rows(which * n_q + q, piece)
        scattered[own, :] = part[own, :]

    per = width // cut
    for which in range(per):
        span = slice(which * cut, (which + 1) * cut)
        part[span, :] = dot(feat_t[span, :], dpre).astype(BF)
        scatter(which)
    agg_t = agg.astype(F32).T.astype(BF)
    for which in range(per):
        span = slice(which * cut, (which + 1) * cut)
        part[width + which * cut : width + (which + 1) * cut, :] = dot(
            agg_t[span, :], dpre
        ).astype(BF)
        scatter(per + which)

    dagg = dot_nt(dpre, wnbr_ref[...]) * (1.0 / fan)
    dagg_high, dagg_low = split(dagg)

    def spread(start, stop):
        held = onehot[start:stop, :]
        return dot(held, dagg_high) + dot(held, dagg_low)

    hub_wide = spread(hub_base, hub_base + owners * hub2)
    hub_wide = jnp.where(hub_half, hub_wide[:, :half], hub_wide[:, half:])
    back_hub[...] = hub_wide.reshape(n_q, n_hi, hub2, half).astype(BF)

    def send_back(step):
        peer, device = near(step)
        copy(back_hub.at[peer], ret_hub.at[q], BACK_NEAR, device)

    loop(n_q, send_back)
    ret_hub[q] = back_hub[q]
    back_border[...] = spread(nodes, hub_base).astype(BF)
    to_members(back_border, ret_border, BACK_BORDER)

    near_rows = (n_q - 1) * piece
    line_rows = (n_hi - 1) * piece

    def cross(which):
        wait_bytes(scattered.at[pl.ds(which * cut, near_rows)], recv_sem.at[SCATTER + which])
        summed = jnp.zeros((piece, width), F32)
        for index in range(n_q):
            start = which * cut + index * piece
            summed = summed + scattered[start : start + piece, :].astype(F32)
        source = mine.at[pl.ds(which * piece, piece)]
        source[...] = summed.astype(BF)
        slot = rows(which * n_hi + hi, piece)
        loop(n_hi, lambda step: copy(source, across.at[slot], CROSS + which, line(step)[1]))
        across[slot, :] = source[...]

    for which in range(CUTS):
        cross(which)

    total = dot_nt(dpre, wself_ref[...]) + spread(0, nodes)

    wait_bytes(ret_hub.at[pl.ds(0, n_q - 1)], recv_sem.at[BACK_NEAR])
    line_back[...] = jnp.sum(ret_hub[...].astype(F32), axis=0).astype(BF)

    def send_line(step):
        peer, device = line(step)
        copy(line_back.at[peer], line_ret.at[hi], BACK_LINE, device)

    loop(n_hi, send_line)
    line_ret[hi] = line_back[hi]

    def gather(which):
        first = which * n_hi
        wait_bytes(across.at[pl.ds(first * piece, line_rows)], recv_sem.at[CROSS + which])
        summed = lax.fori_loop(
            0,
            n_hi,
            lambda index, carry: carry + across[rows(first + index, piece), :].astype(F32),
            jnp.zeros((piece, width), F32),
            unroll=n_hi <= 16,
        )
        source = reduced.at[pl.ds(which * piece, piece)]
        source[...] = summed.astype(BF)
        slot = rows(which * n_q + q, piece)
        loop(n_q, lambda step: copy(source, out_ref.at[slot], GATHER + which, near(step)[1]))
        out_ref[slot, :] = source[...]

    for which in range(CUTS):
        gather(which)

    wait_bytes(ret_border.at[pl.ds(0, others)], recv_sem.at[BACK_BORDER])
    total = total + dot(pick[:, :border_rows], ret_border[...])
    wait_bytes(line_ret.at[pl.ds(0, n_hi - 1)], recv_sem.at[BACK_LINE])
    hub_sum = jnp.sum(line_ret[...].astype(F32), axis=0)
    top = lane_row < hubs
    hub_sum = jnp.concatenate(
        [jnp.where(top, hub_sum, zero), jnp.where(top, zero, hub_sum)], axis=1
    )
    hub_high, hub_low = split(hub_sum)
    hub_back = jnp.concatenate(
        [
            hub_high.astype(F32),
            hub_low.astype(F32),
            jnp.zeros((128 - 2 * hub2, width), F32),
        ],
        axis=0,
    ).astype(BF)
    out_ref[2 * width :, :] = (total + dot(pick[:, border_rows:], hub_back)).astype(BF)

    wait_bytes(out_border.at[pl.ds(0, others)], send_sem.at[BORDER])
    wait_bytes(line_hub.at[pl.ds(0, n_hi - 1)], send_sem.at[HUB_LINE])
    wait_bytes(in_hub.at[pl.ds(0, n_q - 1)], send_sem.at[HUB_NEAR])
    wait_bytes(back_border.at[pl.ds(0, others)], send_sem.at[BACK_BORDER])
    wait_bytes(back_hub.at[pl.ds(0, n_q - 1)], send_sem.at[BACK_NEAR])
    wait_bytes(line_back.at[pl.ds(0, n_hi - 1)], send_sem.at[BACK_LINE])
    for which in range(CUTS):
        wait_bytes(part.at[pl.ds(which * cut, near_rows)], send_sem.at[SCATTER + which])
        wait_bytes(across.at[pl.ds(which * n_hi * piece, line_rows)], send_sem.at[CROSS + which])
    for which in range(CUTS):
        wait_bytes(out_ref.at[pl.ds(which * cut, near_rows)], recv_sem.at[GATHER + which])
        wait_bytes(part.at[pl.ds(which * cut, near_rows)], send_sem.at[GATHER + which])


def finish(scale, held_ref, self_hbm, nbr_hbm, feat_hbm, stage, sems):
    width = stage.shape[0] // 2
    copies = [pltpu.make_async_copy(held_ref.at[pl.ds(2 * width, feat_hbm.shape[0])], feat_hbm, sems.at[2])]
    copies[0].start()
    for index, target in enumerate((self_hbm, nbr_hbm)):
        span = pl.ds(index * width, width)
        stage[span, :] = held_ref[span, :].astype(F32) * scale
        copies.append(pltpu.make_async_copy(stage.at[span], target, sems.at[index]))
        copies[-1].start()
    for copy in copies:
        copy.wait()


def local(features, neighbours, send_rows, block_counts, hub_rows, w_self, w_nbr, cotangent):
    nodes, width = features.shape
    n_member = lax.axis_size("member")
    n_group = lax.axis_size("group")
    block = send_rows.shape[1]
    hubs = hub_rows.shape[1]
    owners = n_group * n_member
    hub2 = 2 * hubs
    low = max(1, 8 // n_group)
    n_q = n_group * low
    n_hi = n_member // low
    piece = 2 * width // (CUTS * n_q)
    half = width // 2
    border_rows = n_member * block
    table_rows = nodes + border_rows + owners * hub2
    border = pltpu.VMEM((border_rows, width), BF)
    hub_line = pltpu.VMEM((n_hi, hub2, half), BF)
    hub_all = pltpu.VMEM((n_q, n_hi, hub2, half), BF)
    pair = pltpu.VMEM((2 * width, width), BF)
    result = pl.pallas_call(
        functools.partial(kernel, n_group, n_member, low, block, hubs),
        out_shape=pltpu.VMEM((2 * width + nodes, width), BF),
        in_specs=[pl.BlockSpec(memory_space=pltpu.HBM)] * 8,
        out_specs=pl.BlockSpec(memory_space=pltpu.VMEM),
        scratch_shapes=[
            pltpu.VMEM((nodes, width), BF),
            pltpu.VMEM((neighbours.shape[1], nodes), jnp.int32),
            pltpu.VMEM(send_rows.shape, jnp.int32),
            pltpu.VMEM((1, n_member), jnp.int32),
            pltpu.VMEM(hub_rows.shape, jnp.int32),
            pltpu.VMEM((width, width), BF),
            pltpu.VMEM((width, width), BF),
            pltpu.VMEM((nodes, width), BF),
            pltpu.SemaphoreType.DMA((8,)),
            pltpu.VMEM((table_rows, nodes), BF),
            pltpu.VMEM((nodes, table_rows), BF),
            border,
            border,
            pltpu.VMEM((hub2, half), BF),
            hub_line,
            hub_all,
            border,
            border,
            hub_all,
            hub_all,
            hub_line,
            hub_line,
            pair,
            pair,
            pltpu.VMEM((CUTS * piece, width), BF),
            pltpu.VMEM((CUTS * n_hi * piece, width), BF),
            pltpu.VMEM((CUTS * piece, width), BF),
            pltpu.SemaphoreType.DMA((SEMS,)),
            pltpu.SemaphoreType.DMA((SEMS,)),
        ],
        compiler_params=pltpu.CompilerParams(
            collective_id=0, has_side_effects=True, vmem_limit_bytes=60 * 1024 * 1024
        ),
    )(
        features,
        neighbours.T,
        send_rows,
        block_counts.reshape(1, -1),
        hub_rows,
        w_self,
        w_nbr,
        cotangent,
    )
    scale = 1.0 / math.sqrt(nodes * owners)
    full = jax.ShapeDtypeStruct((width, width), F32)
    return pl.pallas_call(
        functools.partial(finish, scale),
        out_shape=(full, full, jax.ShapeDtypeStruct((nodes, width), BF)),
        in_specs=[pl.BlockSpec(memory_space=pltpu.VMEM)],
        out_specs=(pl.BlockSpec(memory_space=pl.ANY),) * 3,
        scratch_shapes=[pltpu.VMEM((2 * width, width), F32), pltpu.SemaphoreType.DMA((3,))],
    )(result)


def solution(mesh):
    in_specs = (
        P(("group", "member"), None),
        P(("group", "member"), None),
        P(("group", "member"), None),
        P(("group", "member")),
        P(("group", "member"), None),
        P(),
        P(),
        P(("group", "member"), None),
    )
    out_specs = (P(), P(), P(("group", "member"), None))
    return jax.shard_map(local, mesh=mesh, in_specs=in_specs, out_specs=out_specs, check_vma=False)
```

```python
import functools
import math

import jax
import jax.numpy as jnp
from jax import lax
from jax.experimental import pallas as pl
from jax.experimental.pallas import tpu as pltpu
from jax.sharding import PartitionSpec as P

MESH = pl.DeviceIdType.MESH
BF = jnp.bfloat16
F32 = jnp.float32
CHUNK = 256
CUTS = 2
BORDER, HUB_LINE, HUB_NEAR, BACK_BORDER, BACK_NEAR, BACK_LINE = range(6)
SCATTER, CROSS, GATHER = 6, 6 + CUTS, 6 + 2 * CUTS
SEMS = 6 + 3 * CUTS


def dot(a, b):
    return jnp.dot(a, b, preferred_element_type=F32)


def dot_tn(a, b):
    return lax.dot_general(a, b, (((0,), (0,)), ((), ())), preferred_element_type=F32)


def dot_nt(a, b):
    return lax.dot_general(a, b, (((1,), (1,)), ((), ())), preferred_element_type=F32)


def split(value):
    high = value.astype(BF)
    return high, (value - high.astype(F32)).astype(BF)


def wait_bytes(ref, sem):
    pltpu.make_async_copy(ref, ref, sem).wait()


def select_rows(n_member, block, send_rows, counts):
    lanes = n_member * block
    lane = lax.broadcasted_iota(jnp.int32, (n_member, lanes), 1)
    peer = lax.broadcasted_iota(jnp.int32, (n_member, lanes), 0)
    own = lane // block == peer
    slot = lax.broadcasted_iota(jnp.int32, (block, lanes), 0)
    slot_lane = lax.broadcasted_iota(jnp.int32, (block, lanes), 1) % block
    expand = jnp.where(slot == slot_lane, 1.0, 0.0).astype(BF)
    spread_rows = dot(send_rows.astype(F32).astype(BF), expand)
    row = jnp.sum(jnp.where(own, spread_rows, 0.0), axis=0, keepdims=True)
    repeat = jnp.where(own, 1.0, 0.0).astype(BF)
    counts = jnp.broadcast_to(counts.astype(F32), (8, n_member)).astype(BF)
    live = dot(counts, repeat)[:1].astype(jnp.int32)
    lane = lax.broadcasted_iota(jnp.int32, (1, lanes), 1)
    return jnp.where(lane % block < live, row.astype(jnp.int32), -1)


def select_hubs(hubs, hub_rows):
    lane = lax.broadcasted_iota(jnp.int32, (hubs, 128), 1)
    hub = lax.broadcasted_iota(jnp.int32, (hubs, 128), 0)
    repeat = jnp.where(lane % hubs == hub, 1.0, 0.0).astype(BF)
    wide = jnp.broadcast_to(hub_rows.astype(F32), (8, hubs)).astype(BF)
    row = dot(wide, repeat)[:1].astype(jnp.int32)
    lane = lax.broadcasted_iota(jnp.int32, (1, 128), 1)
    return jnp.where(lane < 4 * hubs, row, -1)


def kernel(
    n_group,
    n_member,
    low,
    block,
    hubs,
    feat_hbm,
    nbr_hbm,
    rows_hbm,
    counts_hbm,
    hubs_hbm,
    wself_hbm,
    wnbr_hbm,
    cot_hbm,
    out_ref,
    feat_ref,
    nbr_ref,
    rows_ref,
    counts_ref,
    hubs_ref,
    wself_ref,
    wnbr_ref,
    cot_ref,
    load_sem,
    onehot,
    onehot_t,
    out_border,
    in_border,
    out_hub,
    line_hub,
    in_hub,
    back_border,
    ret_border,
    back_hub,
    ret_hub,
    line_back,
    line_ret,
    part,
    scattered,
    mine,
    across,
    reduced,
    landed,
    send_sem,
    recv_sem,
):
    nodes, width = feat_ref.shape
    half = width // 2
    fan = nbr_ref.shape[0]
    owners = n_group * n_member
    hub2 = 2 * hubs
    border_rows = n_member * block
    hub_base = nodes + border_rows
    g = lax.axis_index("group")
    m = lax.axis_index("member")
    hi, lo = lax.div(m, low), lax.rem(m, low)
    n_hi = n_member // low
    n_q = n_group * low
    q = g * low + lo
    piece = 2 * width // (CUTS * n_q)
    cut = n_q * piece

    loads = [
        pltpu.make_async_copy(src, dst, load_sem.at[index])
        for index, (src, dst) in enumerate(
            (
                (rows_hbm, rows_ref),
                (counts_hbm, counts_ref),
                (hubs_hbm, hubs_ref),
                (feat_hbm, feat_ref),
                (nbr_hbm, nbr_ref),
                (wself_hbm, wself_ref),
                (wnbr_hbm, wnbr_ref),
                (cot_hbm, cot_ref),
            )
        )
    ]
    for load in loads:
        load.start()

    def loop(count, body):
        lax.fori_loop(1, count, lambda step, carry: (body(step), carry)[1], 0, unroll=count <= 16)

    def member(step):
        down, up = n_member - step, step - 1
        down = jnp.where(down > m, down, down - 1)
        up = jnp.where(up < m, up, up + 1)
        peer = jnp.where(m < n_member // 2, down, up)
        return peer, (g, peer)

    def near(step):
        peer = lax.rem(q + step, n_q)
        return peer, (lax.div(peer, low), hi * low + lax.rem(peer, low))

    def line(step):
        peer = lax.rem(hi + step, n_hi)
        return peer, (g, peer * low + lo)

    barrier = pltpu.get_barrier_semaphore()

    def greet(device):
        pl.semaphore_signal(barrier, inc=1, device_id=device, device_id_type=MESH)

    loop(n_member, lambda step: greet(member(step)[1]))
    for step in range(1, n_group):
        for other in range(low):
            greet((lax.rem(g + step, n_group), hi * low + other))

    def copy(src, dst, which, device):
        pltpu.make_async_remote_copy(
            src_ref=src,
            dst_ref=dst,
            send_sem=send_sem.at[which],
            recv_sem=recv_sem.at[which],
            device_id=device,
            device_id_type=MESH,
        ).start()

    def rows(start, count):
        return pl.ds(pl.multiple_of(start * count, count), count)

    def to_members(src, dst, which):
        def body(step):
            peer, device = member(step)
            copy(src.at[rows(peer, block)], dst.at[rows(m, block)], which, device)

        loop(n_member, body)
        dst[rows(m, block), :] = src[rows(m, block), :]

    for load in loads[:3]:
        load.wait()
    sel_rows = select_rows(n_member, block, rows_ref[...], counts_ref[...])
    sel = jnp.concatenate([sel_rows, select_hubs(hubs, hubs_ref[...])], axis=1)
    row_of = lax.broadcasted_iota(jnp.int32, (nodes, border_rows + 128), 0)
    pick = jnp.where(row_of == sel, 1.0, 0.0).astype(BF)
    loads[3].wait()
    feat = feat_ref[...]
    picked = dot_tn(pick, feat)
    out_border[...] = picked[:border_rows].astype(BF)
    hub_wide = picked[border_rows : border_rows + hub2]
    lane_row = lax.broadcasted_iota(jnp.int32, (hub2, half), 0)
    out_hub[...] = jnp.where(lane_row < hubs, hub_wide[:, :half], hub_wide[:, half:]).astype(BF)

    pl.semaphore_wait(barrier, n_member - 1 + (n_group - 1) * low)

    loop(n_hi, lambda step: copy(out_hub, line_hub.at[hi], HUB_LINE, line(step)[1]))
    line_hub[hi] = out_hub[...]
    to_members(out_border, in_border, BORDER)

    for load in loads[4:]:
        load.wait()

    def count(names):
        names = jnp.concatenate([names] * (nodes // 128), axis=1)
        total = jnp.zeros((CHUNK, nodes), F32)
        for sample in range(fan):
            total = total + jnp.where(names == nbr_ref[sample : sample + 1, :], 1.0, 0.0)
        return total

    def chunk_names(index):
        return lax.broadcasted_iota(jnp.int32, (CHUNK, 128), 0) + index * CHUNK

    def store(index, total):
        onehot[rows(index, CHUNK), :] = total.astype(BF)
        onehot_t[:, rows(index, CHUNK)] = total.T.astype(BF)

    plain_chunks = hub_base // CHUNK
    hub_chunks = owners * hub2 // CHUNK

    def fill_plain(index, carry):
        store(index, count(chunk_names(index)))
        return carry

    def fill_hub(index, carry):
        row = chunk_names(index)
        slab = lax.div(row, hub2)
        near_id = lax.div(slab, n_hi)
        owner = (
            lax.div(near_id, low) * n_member + lax.rem(slab, n_hi) * low + lax.rem(near_id, low)
        )
        store(plain_chunks + index, count(hub_base + owner * hubs + lax.rem(row, hubs)))
        return carry

    fill_plain(0, 0)

    wait_bytes(line_hub.at[pl.ds(0, n_hi - 1)], recv_sem.at[HUB_LINE])
    loop(n_q, lambda step: copy(line_hub, in_hub.at[q], HUB_NEAR, near(step)[1]))
    in_hub[q] = line_hub[...]

    lax.fori_loop(1, plain_chunks, fill_plain, 0)
    lax.fori_loop(0, hub_chunks, fill_hub, 0)
    pre_self = dot(feat, wself_ref[...])
    agg_sum = dot(onehot_t[:, :nodes], feat)
    feat_t = feat.astype(F32).T.astype(BF)

    wait_bytes(in_hub.at[pl.ds(0, n_q - 1)], recv_sem.at[HUB_NEAR])
    hub_half = lax.broadcasted_iota(jnp.int32, (owners * hub2, half), 0) % hub2 < hubs
    hub_rows = in_hub[...].astype(F32).reshape(owners * hub2, half)
    zero = jnp.zeros((), F32)
    hub_table = jnp.concatenate(
        [jnp.where(hub_half, hub_rows, zero), jnp.where(hub_half, zero, hub_rows)], axis=1
    ).astype(BF)
    agg_sum = agg_sum + dot(onehot_t[:, hub_base:], hub_table)
    others = (n_member - 1) * block
    wait_bytes(in_border.at[pl.ds(0, others)], recv_sem.at[BORDER])
    agg_sum = agg_sum + dot(onehot_t[:, nodes:hub_base], in_border[...])
    agg = (agg_sum * (1.0 / fan)).astype(BF)

    pre = pre_self + dot(agg, wnbr_ref[...])
    sigma = 0.5 * jnp.tanh(0.5 * pre) + 0.5
    dpre = (cot_ref[...].astype(F32) * sigma * (1.0 + pre * (1.0 - sigma))).astype(BF)

    def scatter(which):
        def body(step):
            peer, device = near(step)
            copy(
                part.at[rows(which * n_q + peer, piece)],
                scattered.at[rows(which * n_q + q, piece)],
                SCATTER + which,
                device,
            )

        loop(n_q, body)
        own = rows(which * n_q + q, piece)
        scattered[own, :] = part[own, :]

    per = width // cut
    for which in range(per):
        span = slice(which * cut, (which + 1) * cut)
        part[span, :] = dot(feat_t[span, :], dpre).astype(BF)
        scatter(which)
    agg_t = agg.astype(F32).T.astype(BF)
    for which in range(per):
        span = slice(which * cut, (which + 1) * cut)
        part[width + which * cut : width + (which + 1) * cut, :] = dot(
            agg_t[span, :], dpre
        ).astype(BF)
        scatter(per + which)

    dagg = dot_nt(dpre, wnbr_ref[...]) * (1.0 / fan)
    dagg = dagg.astype(BF)

    def spread(start, stop):
        return dot(onehot[start:stop, :], dagg)

    hub_wide = spread(hub_base, hub_base + owners * hub2)
    hub_wide = jnp.where(hub_half, hub_wide[:, :half], hub_wide[:, half:])
    back_hub[...] = hub_wide.reshape(n_q, n_hi, hub2, half).astype(BF)

    def send_back(step):
        peer, device = near(step)
        copy(back_hub.at[peer], ret_hub.at[q], BACK_NEAR, device)

    loop(n_q, send_back)
    ret_hub[q] = back_hub[q]
    back_border[...] = spread(nodes, hub_base).astype(BF)
    to_members(back_border, ret_border, BACK_BORDER)

    near_rows = (n_q - 1) * piece
    line_rows = (n_hi - 1) * piece

    def cross(which):
        wait_bytes(scattered.at[pl.ds(which * cut, near_rows)], recv_sem.at[SCATTER + which])
        summed = jnp.zeros((piece, width), F32)
        for index in range(n_q):
            start = which * cut + index * piece
            summed = summed + scattered[start : start + piece, :].astype(F32)
        source = mine.at[pl.ds(which * piece, piece)]
        source[...] = summed.astype(BF)
        slot = rows(which * n_hi + hi, piece)
        loop(n_hi, lambda step: copy(source, across.at[slot], CROSS + which, line(step)[1]))
        across[slot, :] = source[...]

    for which in range(CUTS):
        cross(which)

    total = dot_nt(dpre, wself_ref[...]) + spread(0, nodes)

    wait_bytes(ret_hub.at[pl.ds(0, n_q - 1)], recv_sem.at[BACK_NEAR])
    line_back[...] = jnp.sum(ret_hub[...].astype(F32), axis=0).astype(BF)

    def send_line(step):
        peer, device = line(step)
        copy(line_back.at[peer], line_ret.at[hi], BACK_LINE, device)

    loop(n_hi, send_line)
    line_ret[hi] = line_back[hi]

    def gather(which):
        first = which * n_hi
        wait_bytes(across.at[pl.ds(first * piece, line_rows)], recv_sem.at[CROSS + which])
        summed = lax.fori_loop(
            0,
            n_hi,
            lambda index, carry: carry + across[rows(first + index, piece), :].astype(F32),
            jnp.zeros((piece, width), F32),
            unroll=n_hi <= 16,
        )
        source = reduced.at[pl.ds(which * piece, piece)]
        source[...] = summed.astype(BF)
        slot = rows(which * n_q + q, piece)
        loop(n_q, lambda step: copy(source, landed.at[slot], GATHER + which, near(step)[1]))
        landed[slot, :] = source[...]

    for which in range(CUTS):
        gather(which)

    wait_bytes(ret_border.at[pl.ds(0, others)], recv_sem.at[BACK_BORDER])
    total = total + dot(pick[:, :border_rows], ret_border[...])
    wait_bytes(line_ret.at[pl.ds(0, n_hi - 1)], recv_sem.at[BACK_LINE])
    hub_sum = jnp.sum(line_ret[...].astype(F32), axis=0)
    top = lane_row < hubs
    hub_sum = jnp.concatenate(
        [jnp.where(top, hub_sum, zero), jnp.where(top, zero, hub_sum)], axis=1
    )
    hub_high, hub_low = split(hub_sum)
    hub_back = jnp.concatenate(
        [
            hub_high.astype(F32),
            hub_low.astype(F32),
            jnp.zeros((128 - 2 * hub2, width), F32),
        ],
        axis=0,
    ).astype(BF)
    out_ref[2 * width :, :] = 2.0 * (total + dot(pick[:, border_rows:], hub_back))

    wait_bytes(out_border.at[pl.ds(0, others)], send_sem.at[BORDER])
    wait_bytes(line_hub.at[pl.ds(0, n_hi - 1)], send_sem.at[HUB_LINE])
    wait_bytes(in_hub.at[pl.ds(0, n_q - 1)], send_sem.at[HUB_NEAR])
    wait_bytes(back_border.at[pl.ds(0, others)], send_sem.at[BACK_BORDER])
    wait_bytes(back_hub.at[pl.ds(0, n_q - 1)], send_sem.at[BACK_NEAR])
    wait_bytes(line_back.at[pl.ds(0, n_hi - 1)], send_sem.at[BACK_LINE])
    for which in range(CUTS):
        wait_bytes(part.at[pl.ds(which * cut, near_rows)], send_sem.at[SCATTER + which])
        wait_bytes(across.at[pl.ds(which * n_hi * piece, line_rows)], send_sem.at[CROSS + which])
    for which in range(CUTS):
        wait_bytes(landed.at[pl.ds(which * cut, near_rows)], recv_sem.at[GATHER + which])
        span = slice(which * cut, (which + 1) * cut)
        out_ref[span, :] = landed[span, :].astype(F32)
        wait_bytes(part.at[pl.ds(which * cut, near_rows)], send_sem.at[GATHER + which])


def local(features, neighbours, send_rows, block_counts, hub_rows, w_self, w_nbr, cotangent):
    nodes, width = features.shape
    n_member = lax.axis_size("member")
    n_group = lax.axis_size("group")
    block = send_rows.shape[1]
    hubs = hub_rows.shape[1]
    owners = n_group * n_member
    hub2 = 2 * hubs
    low = max(1, 8 // n_group)
    n_q = n_group * low
    n_hi = n_member // low
    piece = 2 * width // (CUTS * n_q)
    half = width // 2
    border_rows = n_member * block
    table_rows = nodes + border_rows + owners * hub2
    border = pltpu.VMEM((border_rows, width), BF)
    hub_line = pltpu.VMEM((n_hi, hub2, half), BF)
    hub_all = pltpu.VMEM((n_q, n_hi, hub2, half), BF)
    pair = pltpu.VMEM((2 * width, width), BF)
    result = pl.pallas_call(
        functools.partial(kernel, n_group, n_member, low, block, hubs),
        out_shape=pltpu.VMEM((2 * width + nodes, width), F32),
        in_specs=[pl.BlockSpec(memory_space=pltpu.HBM)] * 8,
        out_specs=pl.BlockSpec(memory_space=pltpu.VMEM),
        scratch_shapes=[
            pltpu.VMEM((nodes, width), BF),
            pltpu.VMEM((neighbours.shape[1], nodes), jnp.int32),
            pltpu.VMEM(send_rows.shape, jnp.int32),
            pltpu.VMEM((1, n_member), jnp.int32),
            pltpu.VMEM(hub_rows.shape, jnp.int32),
            pltpu.VMEM((width, width), BF),
            pltpu.VMEM((width, width), BF),
            pltpu.VMEM((nodes, width), BF),
            pltpu.SemaphoreType.DMA((8,)),
            pltpu.VMEM((table_rows, nodes), BF),
            pltpu.VMEM((nodes, table_rows), BF),
            border,
            border,
            pltpu.VMEM((hub2, half), BF),
            hub_line,
            hub_all,
            border,
            border,
            hub_all,
            hub_all,
            hub_line,
            hub_line,
            pair,
            pair,
            pltpu.VMEM((CUTS * piece, width), BF),
            pltpu.VMEM((CUTS * n_hi * piece, width), BF),
            pltpu.VMEM((CUTS * piece, width), BF),
            pair,
            pltpu.SemaphoreType.DMA((SEMS,)),
            pltpu.SemaphoreType.DMA((SEMS,)),
        ],
        compiler_params=pltpu.CompilerParams(
            collective_id=0, has_side_effects=True, vmem_limit_bytes=60 * 1024 * 1024
        ),
    )(
        features,
        neighbours.T,
        send_rows,
        block_counts.reshape(1, -1),
        hub_rows,
        w_self,
        w_nbr,
        cotangent,
    )
    scale = 1.0 / math.sqrt(nodes * owners)
    grad_self = result[:width] * scale
    grad_nbr = result[width : 2 * width] * scale
    return (grad_self, grad_nbr, (0.5 * result[2 * width :]).astype(BF))


def solution(mesh):
    in_specs = (
        P(("group", "member"), None),
        P(("group", "member"), None),
        P(("group", "member"), None),
        P(("group", "member")),
        P(("group", "member"), None),
        P(),
        P(),
        P(("group", "member"), None),
    )
    out_specs = (P(), P(), P(("group", "member"), None))
    return jax.shard_map(local, mesh=mesh, in_specs=in_specs, out_specs=out_specs, check_vma=False)
```

```python
import functools
import math

import jax
import jax.numpy as jnp
from jax import lax
from jax.experimental import pallas as pl
from jax.experimental.pallas import tpu as pltpu
from jax.sharding import PartitionSpec as P

MESH = pl.DeviceIdType.MESH
BF = jnp.bfloat16
F32 = jnp.float32
CHUNK = 128
CUTS = 2
BORDER, HUB_LINE, HUB_NEAR, BACK_BORDER, BACK_NEAR, BACK_LINE = range(6)
SCATTER, CROSS, GATHER = 6, 6 + CUTS, 6 + 2 * CUTS
SEMS = 6 + 3 * CUTS


def dot(a, b):
    return jnp.dot(a, b, preferred_element_type=F32)


def dot_tn(a, b):
    return lax.dot_general(a, b, (((0,), (0,)), ((), ())), preferred_element_type=F32)


def dot_nt(a, b):
    return lax.dot_general(a, b, (((1,), (1,)), ((), ())), preferred_element_type=F32)


def split(value):
    high = value.astype(BF)
    return high, (value - high.astype(F32)).astype(BF)


def wait_bytes(ref, sem):
    pltpu.make_async_copy(ref, ref, sem).wait()


def select_rows(n_member, block, send_rows, counts):
    lanes = n_member * block
    lane = lax.broadcasted_iota(jnp.int32, (n_member, lanes), 1)
    peer = lax.broadcasted_iota(jnp.int32, (n_member, lanes), 0)
    own = lane // block == peer
    slot = lax.broadcasted_iota(jnp.int32, (block, lanes), 0)
    slot_lane = lax.broadcasted_iota(jnp.int32, (block, lanes), 1) % block
    expand = jnp.where(slot == slot_lane, 1.0, 0.0).astype(BF)
    spread_rows = dot(send_rows.astype(F32).astype(BF), expand)
    row = jnp.sum(jnp.where(own, spread_rows, 0.0), axis=0, keepdims=True)
    repeat = jnp.where(own, 1.0, 0.0).astype(BF)
    counts = jnp.broadcast_to(counts.astype(F32), (8, n_member)).astype(BF)
    live = dot(counts, repeat)[:1].astype(jnp.int32)
    lane = lax.broadcasted_iota(jnp.int32, (1, lanes), 1)
    return jnp.where(lane % block < live, row.astype(jnp.int32), -1)


def select_hubs(hubs, hub_rows):
    lane = lax.broadcasted_iota(jnp.int32, (hubs, 128), 1)
    hub = lax.broadcasted_iota(jnp.int32, (hubs, 128), 0)
    repeat = jnp.where(lane % hubs == hub, 1.0, 0.0).astype(BF)
    wide = jnp.broadcast_to(hub_rows.astype(F32), (8, hubs)).astype(BF)
    row = dot(wide, repeat)[:1].astype(jnp.int32)
    lane = lax.broadcasted_iota(jnp.int32, (1, 128), 1)
    return jnp.where(lane < 4 * hubs, row, -1)


def kernel(
    n_group,
    n_member,
    low,
    block,
    hubs,
    feat_hbm,
    nbr_hbm,
    rows_hbm,
    counts_hbm,
    hubs_hbm,
    wself_hbm,
    wnbr_hbm,
    cot_hbm,
    out_ref,
    feat_ref,
    nbr_ref,
    rows_ref,
    counts_ref,
    hubs_ref,
    wself_ref,
    wnbr_ref,
    cot_ref,
    load_sem,
    onehot,
    onehot_t,
    out_border,
    in_border,
    out_hub,
    line_hub,
    in_hub,
    back_border,
    ret_border,
    back_hub,
    ret_hub,
    line_back,
    line_ret,
    part,
    scattered,
    mine,
    across,
    reduced,
    landed,
    send_sem,
    recv_sem,
):
    nodes, width = feat_ref.shape
    half = width // 2
    fan = nbr_ref.shape[0]
    owners = n_group * n_member
    hub2 = 2 * hubs
    border_rows = n_member * block
    hub_base = nodes + border_rows
    g = lax.axis_index("group")
    m = lax.axis_index("member")
    hi, lo = lax.div(m, low), lax.rem(m, low)
    n_hi = n_member // low
    n_q = n_group * low
    q = g * low + lo
    piece = 2 * width // (CUTS * n_q)
    cut = n_q * piece

    loads = [
        pltpu.make_async_copy(src, dst, load_sem.at[index])
        for index, (src, dst) in enumerate(
            (
                (rows_hbm, rows_ref),
                (counts_hbm, counts_ref),
                (hubs_hbm, hubs_ref),
                (feat_hbm, feat_ref),
                (nbr_hbm, nbr_ref),
                (wself_hbm, wself_ref),
                (wnbr_hbm, wnbr_ref),
                (cot_hbm, cot_ref),
            )
        )
    ]
    for load in loads:
        load.start()

    def loop(count, body):
        lax.fori_loop(1, count, lambda step, carry: (body(step), carry)[1], 0)

    def member(step):
        down, up = n_member - step, step - 1
        down = jnp.where(down > m, down, down - 1)
        up = jnp.where(up < m, up, up + 1)
        peer = jnp.where(m < n_member // 2, down, up)
        return peer, (g, peer)

    def near(step):
        peer = lax.rem(q + step, n_q)
        return peer, (lax.div(peer, low), hi * low + lax.rem(peer, low))

    def line(step):
        peer = lax.rem(hi + step, n_hi)
        return peer, (g, peer * low + lo)

    barrier = pltpu.get_barrier_semaphore()

    def greet(device):
        pl.semaphore_signal(barrier, inc=1, device_id=device, device_id_type=MESH)

    loop(n_member, lambda step: greet(member(step)[1]))
    for step in range(1, n_group):
        for other in range(low):
            greet((lax.rem(g + step, n_group), hi * low + other))

    def copy(src, dst, which, device):
        pltpu.make_async_remote_copy(
            src_ref=src,
            dst_ref=dst,
            send_sem=send_sem.at[which],
            recv_sem=recv_sem.at[which],
            device_id=device,
            device_id_type=MESH,
        ).start()

    def rows(start, count):
        return pl.ds(pl.multiple_of(start * count, count), count)

    def to_members(src, dst, which):
        def body(step):
            peer, device = member(step)
            copy(src.at[rows(peer, block)], dst.at[rows(m, block)], which, device)

        loop(n_member, body)
        dst[rows(m, block), :] = src[rows(m, block), :]

    for load in loads[:3]:
        load.wait()
    sel_rows = select_rows(n_member, block, rows_ref[...], counts_ref[...])
    sel = jnp.concatenate([sel_rows, select_hubs(hubs, hubs_ref[...])], axis=1)
    row_of = lax.broadcasted_iota(jnp.int32, (nodes, border_rows + 128), 0)
    pick = jnp.where(row_of == sel, 1.0, 0.0).astype(BF)
    loads[3].wait()
    feat = feat_ref[...]
    picked = dot_tn(pick, feat)
    out_border[...] = picked[:border_rows].astype(BF)
    hub_wide = picked[border_rows : border_rows + hub2]
    lane_row = lax.broadcasted_iota(jnp.int32, (hub2, half), 0)
    out_hub[...] = jnp.where(lane_row < hubs, hub_wide[:, :half], hub_wide[:, half:]).astype(BF)

    pl.semaphore_wait(barrier, n_member - 1 + (n_group - 1) * low)

    loop(n_hi, lambda step: copy(out_hub, line_hub.at[hi], HUB_LINE, line(step)[1]))
    line_hub[hi] = out_hub[...]
    to_members(out_border, in_border, BORDER)

    for load in loads[4:]:
        load.wait()

    def count(names):
        names = jnp.concatenate([names] * (nodes // 128), axis=1)
        total = jnp.zeros((CHUNK, nodes), F32)
        for sample in range(fan):
            total = total + jnp.where(names == nbr_ref[sample : sample + 1, :], 1.0, 0.0)
        return total

    def chunk_names(index):
        return lax.broadcasted_iota(jnp.int32, (CHUNK, 128), 0) + index * CHUNK

    def store(index, total):
        onehot[rows(index, CHUNK), :] = total.astype(BF)
        onehot_t[:, rows(index, CHUNK)] = total.T.astype(BF)

    def fill(index, carry):
        row = chunk_names(index)
        hub_row = row - hub_base
        slab = lax.div(hub_row, hub2)
        near_id = lax.div(slab, n_hi)
        owner = (
            lax.div(near_id, low) * n_member + lax.rem(slab, n_hi) * low + lax.rem(near_id, low)
        )
        hub_name = hub_base + owner * hubs + lax.rem(hub_row, hubs)
        store(index, count(jnp.where(row < hub_base, row, hub_name)))
        return carry

    early = nodes // CHUNK
    lax.fori_loop(0, early, fill, 0)

    wait_bytes(line_hub.at[pl.ds(0, n_hi - 1)], recv_sem.at[HUB_LINE])
    loop(n_q, lambda step: copy(line_hub, in_hub.at[q], HUB_NEAR, near(step)[1]))
    in_hub[q] = line_hub[...]

    lax.fori_loop(early, onehot.shape[0] // CHUNK, fill, 0)
    pre_self = dot(feat, wself_ref[...])
    agg_sum = dot(onehot_t[:, :nodes], feat)
    feat_t = feat.astype(F32).T.astype(BF)

    wait_bytes(in_hub.at[pl.ds(0, n_q - 1)], recv_sem.at[HUB_NEAR])
    hub_half = lax.broadcasted_iota(jnp.int32, (owners * hub2, half), 0) % hub2 < hubs
    hub_rows = in_hub[...].astype(F32).reshape(owners * hub2, half)
    zero = jnp.zeros((), F32)
    hub_table = jnp.concatenate(
        [jnp.where(hub_half, hub_rows, zero), jnp.where(hub_half, zero, hub_rows)], axis=1
    ).astype(BF)
    agg_sum = agg_sum + dot(onehot_t[:, hub_base:], hub_table)
    others = (n_member - 1) * block
    wait_bytes(in_border.at[pl.ds(0, others)], recv_sem.at[BORDER])
    agg_sum = agg_sum + dot(onehot_t[:, nodes:hub_base], in_border[...])
    agg = (agg_sum * (1.0 / fan)).astype(BF)

    pre = pre_self + dot(agg, wnbr_ref[...])
    sigma = 0.5 * jnp.tanh(0.5 * pre) + 0.5
    dpre = (cot_ref[...].astype(F32) * sigma * (1.0 + pre * (1.0 - sigma))).astype(BF)

    def scatter(which):
        def body(step):
            peer, device = near(step)
            copy(
                part.at[rows(which * n_q + peer, piece)],
                scattered.at[rows(which * n_q + q, piece)],
                SCATTER + which,
                device,
            )

        loop(n_q, body)
        own = rows(which * n_q + q, piece)
        scattered[own, :] = part[own, :]

    per = width // cut
    for which in range(per):
        span = slice(which * cut, (which + 1) * cut)
        part[span, :] = dot(feat_t[span, :], dpre).astype(BF)
        scatter(which)
    agg_t = agg.astype(F32).T.astype(BF)
    for which in range(per):
        span = slice(which * cut, (which + 1) * cut)
        part[width + which * cut : width + (which + 1) * cut, :] = dot(
            agg_t[span, :], dpre
        ).astype(BF)
        scatter(per + which)

    dagg = dot_nt(dpre, wnbr_ref[...]) * (1.0 / fan)
    dagg = dagg.astype(BF)

    def spread(start, stop):
        return dot(onehot[start:stop, :], dagg)

    hub_wide = spread(hub_base, hub_base + owners * hub2)
    hub_wide = jnp.where(hub_half, hub_wide[:, :half], hub_wide[:, half:])
    back_hub[...] = hub_wide.reshape(n_q, n_hi, hub2, half).astype(BF)

    def send_back(step):
        peer, device = near(step)
        copy(back_hub.at[peer], ret_hub.at[q], BACK_NEAR, device)

    loop(n_q, send_back)
    ret_hub[q] = back_hub[q]
    back_border[...] = spread(nodes, hub_base).astype(BF)
    to_members(back_border, ret_border, BACK_BORDER)

    near_rows = (n_q - 1) * piece
    line_rows = (n_hi - 1) * piece

    def cross(which):
        wait_bytes(scattered.at[pl.ds(which * cut, near_rows)], recv_sem.at[SCATTER + which])
        summed = jnp.zeros((piece, width), F32)
        for index in range(n_q):
            start = which * cut + index * piece
            summed = summed + scattered[start : start + piece, :].astype(F32)
        source = mine.at[pl.ds(which * piece, piece)]
        source[...] = summed.astype(BF)
        slot = rows(which * n_hi + hi, piece)
        loop(n_hi, lambda step: copy(source, across.at[slot], CROSS + which, line(step)[1]))
        across[slot, :] = source[...]

    for which in range(CUTS):
        cross(which)

    total = dot_nt(dpre, wself_ref[...]) + spread(0, nodes)

    wait_bytes(ret_hub.at[pl.ds(0, n_q - 1)], recv_sem.at[BACK_NEAR])
    line_back[...] = jnp.sum(ret_hub[...].astype(F32), axis=0).astype(BF)

    def send_line(step):
        peer, device = line(step)
        copy(line_back.at[peer], line_ret.at[hi], BACK_LINE, device)

    loop(n_hi, send_line)
    line_ret[hi] = line_back[hi]

    def gather(which):
        first = which * n_hi
        wait_bytes(across.at[pl.ds(first * piece, line_rows)], recv_sem.at[CROSS + which])
        summed = lax.fori_loop(
            0,
            n_hi,
            lambda index, carry: carry + across[rows(first + index, piece), :].astype(F32),
            jnp.zeros((piece, width), F32),
            unroll=n_hi <= 16,
        )
        source = reduced.at[pl.ds(which * piece, piece)]
        source[...] = summed.astype(BF)
        slot = rows(which * n_q + q, piece)
        loop(n_q, lambda step: copy(source, landed.at[slot], GATHER + which, near(step)[1]))
        landed[slot, :] = source[...]

    for which in range(CUTS):
        gather(which)

    wait_bytes(ret_border.at[pl.ds(0, others)], recv_sem.at[BACK_BORDER])
    total = total + dot(pick[:, :border_rows], ret_border[...])
    wait_bytes(line_ret.at[pl.ds(0, n_hi - 1)], recv_sem.at[BACK_LINE])
    hub_sum = jnp.sum(line_ret[...].astype(F32), axis=0)
    top = lane_row < hubs
    hub_sum = jnp.concatenate(
        [jnp.where(top, hub_sum, zero), jnp.where(top, zero, hub_sum)], axis=1
    )
    hub_high, hub_low = split(hub_sum)
    hub_back = jnp.concatenate(
        [
            hub_high.astype(F32),
            hub_low.astype(F32),
            jnp.zeros((128 - 2 * hub2, width), F32),
        ],
        axis=0,
    ).astype(BF)
    out_ref[2 * width :, :] = 2.0 * (total + dot(pick[:, border_rows:], hub_back))

    wait_bytes(out_border.at[pl.ds(0, others)], send_sem.at[BORDER])
    wait_bytes(line_hub.at[pl.ds(0, n_hi - 1)], send_sem.at[HUB_LINE])
    wait_bytes(in_hub.at[pl.ds(0, n_q - 1)], send_sem.at[HUB_NEAR])
    wait_bytes(back_border.at[pl.ds(0, others)], send_sem.at[BACK_BORDER])
    wait_bytes(back_hub.at[pl.ds(0, n_q - 1)], send_sem.at[BACK_NEAR])
    wait_bytes(line_back.at[pl.ds(0, n_hi - 1)], send_sem.at[BACK_LINE])
    for which in range(CUTS):
        wait_bytes(part.at[pl.ds(which * cut, near_rows)], send_sem.at[SCATTER + which])
        wait_bytes(across.at[pl.ds(which * n_hi * piece, line_rows)], send_sem.at[CROSS + which])
    for which in range(CUTS):
        wait_bytes(landed.at[pl.ds(which * cut, near_rows)], recv_sem.at[GATHER + which])
        span = slice(which * cut, (which + 1) * cut)
        out_ref[span, :] = landed[span, :].astype(F32)
        wait_bytes(part.at[pl.ds(which * cut, near_rows)], send_sem.at[GATHER + which])


def local(features, neighbours, send_rows, block_counts, hub_rows, w_self, w_nbr, cotangent):
    nodes, width = features.shape
    n_member = lax.axis_size("member")
    n_group = lax.axis_size("group")
    block = send_rows.shape[1]
    hubs = hub_rows.shape[1]
    owners = n_group * n_member
    hub2 = 2 * hubs
    low = max(1, 8 // n_group)
    n_q = n_group * low
    n_hi = n_member // low
    piece = 2 * width // (CUTS * n_q)
    half = width // 2
    border_rows = n_member * block
    table_rows = nodes + border_rows + owners * hub2
    border = pltpu.VMEM((border_rows, width), BF)
    hub_line = pltpu.VMEM((n_hi, hub2, half), BF)
    hub_all = pltpu.VMEM((n_q, n_hi, hub2, half), BF)
    pair = pltpu.VMEM((2 * width, width), BF)
    result = pl.pallas_call(
        functools.partial(kernel, n_group, n_member, low, block, hubs),
        out_shape=pltpu.VMEM((2 * width + nodes, width), F32),
        in_specs=[pl.BlockSpec(memory_space=pltpu.HBM)] * 8,
        out_specs=pl.BlockSpec(memory_space=pltpu.VMEM),
        scratch_shapes=[
            pltpu.VMEM((nodes, width), BF),
            pltpu.VMEM((neighbours.shape[1], nodes), jnp.int32),
            pltpu.VMEM(send_rows.shape, jnp.int32),
            pltpu.VMEM((1, n_member), jnp.int32),
            pltpu.VMEM(hub_rows.shape, jnp.int32),
            pltpu.VMEM((width, width), BF),
            pltpu.VMEM((width, width), BF),
            pltpu.VMEM((nodes, width), BF),
            pltpu.SemaphoreType.DMA((8,)),
            pltpu.VMEM((table_rows, nodes), BF),
            pltpu.VMEM((nodes, table_rows), BF),
            border,
            border,
            pltpu.VMEM((hub2, half), BF),
            hub_line,
            hub_all,
            border,
            border,
            hub_all,
            hub_all,
            hub_line,
            hub_line,
            pair,
            pair,
            pltpu.VMEM((CUTS * piece, width), BF),
            pltpu.VMEM((CUTS * n_hi * piece, width), BF),
            pltpu.VMEM((CUTS * piece, width), BF),
            pair,
            pltpu.SemaphoreType.DMA((SEMS,)),
            pltpu.SemaphoreType.DMA((SEMS,)),
        ],
        compiler_params=pltpu.CompilerParams(
            collective_id=0, has_side_effects=True, vmem_limit_bytes=60 * 1024 * 1024
        ),
    )(
        features,
        neighbours.T,
        send_rows,
        block_counts.reshape(1, -1),
        hub_rows,
        w_self,
        w_nbr,
        cotangent,
    )
    scale = 1.0 / math.sqrt(nodes * owners)
    grad_self = result[:width] * scale
    grad_nbr = result[width : 2 * width] * scale
    return (grad_self, grad_nbr, (0.5 * result[2 * width :]).astype(BF))


def solution(mesh):
    in_specs = (
        P(("group", "member"), None),
        P(("group", "member"), None),
        P(("group", "member"), None),
        P(("group", "member")),
        P(("group", "member"), None),
        P(),
        P(),
        P(("group", "member"), None),
    )
    out_specs = (P(), P(), P(("group", "member"), None))
    return jax.shard_map(local, mesh=mesh, in_specs=in_specs, out_specs=out_specs, check_vma=False)
```

```python
import functools
import math

import jax
import jax.numpy as jnp
from jax import lax
from jax.experimental import pallas as pl
from jax.experimental.pallas import tpu as pltpu
from jax.sharding import PartitionSpec as P

MESH = pl.DeviceIdType.MESH
BF = jnp.bfloat16
F32 = jnp.float32
CHUNK = 128
CUTS = 2
BORDER, HUB_LINE, HUB_NEAR, BACK_BORDER, BACK_NEAR, BACK_LINE = range(6)
SCATTER, CROSS, GATHER = 6, 6 + CUTS, 6 + 2 * CUTS
SEMS = 6 + 3 * CUTS


def dot(a, b):
    return jnp.dot(a, b, preferred_element_type=F32)


def dot_tn(a, b):
    return lax.dot_general(a, b, (((0,), (0,)), ((), ())), preferred_element_type=F32)


def dot_nt(a, b):
    return lax.dot_general(a, b, (((1,), (1,)), ((), ())), preferred_element_type=F32)


def split(value):
    high = value.astype(BF)
    return high, (value - high.astype(F32)).astype(BF)


def wait_bytes(ref, sem):
    pltpu.make_async_copy(ref, ref, sem).wait()


def select_rows(n_member, block, send_rows, counts):
    lanes = n_member * block
    lane = lax.broadcasted_iota(jnp.int32, (n_member, lanes), 1)
    peer = lax.broadcasted_iota(jnp.int32, (n_member, lanes), 0)
    own = lane // block == peer
    slot = lax.broadcasted_iota(jnp.int32, (block, lanes), 0)
    slot_lane = lax.broadcasted_iota(jnp.int32, (block, lanes), 1) % block
    expand = jnp.where(slot == slot_lane, 1.0, 0.0).astype(BF)
    spread_rows = dot(send_rows.astype(F32).astype(BF), expand)
    row = jnp.sum(jnp.where(own, spread_rows, 0.0), axis=0, keepdims=True)
    repeat = jnp.where(own, 1.0, 0.0).astype(BF)
    counts = jnp.broadcast_to(counts.astype(F32), (8, n_member)).astype(BF)
    live = dot(counts, repeat)[:1].astype(jnp.int32)
    lane = lax.broadcasted_iota(jnp.int32, (1, lanes), 1)
    return jnp.where(lane % block < live, row.astype(jnp.int32), -1)


def select_hubs(hubs, hub_rows):
    lane = lax.broadcasted_iota(jnp.int32, (hubs, 128), 1)
    hub = lax.broadcasted_iota(jnp.int32, (hubs, 128), 0)
    repeat = jnp.where(lane % hubs == hub, 1.0, 0.0).astype(BF)
    wide = jnp.broadcast_to(hub_rows.astype(F32), (8, hubs)).astype(BF)
    row = dot(wide, repeat)[:1].astype(jnp.int32)
    lane = lax.broadcasted_iota(jnp.int32, (1, 128), 1)
    return jnp.where(lane < 4 * hubs, row, -1)


def kernel(
    n_group,
    n_member,
    low,
    block,
    hubs,
    feat_hbm,
    nbr_hbm,
    rows_hbm,
    counts_hbm,
    hubs_hbm,
    wself_hbm,
    wnbr_hbm,
    cot_hbm,
    out_ref,
    feat_ref,
    nbr_ref,
    rows_ref,
    counts_ref,
    hubs_ref,
    wself_ref,
    wnbr_ref,
    cot_ref,
    load_sem,
    onehot,
    onehot_t,
    out_border,
    in_border,
    out_hub,
    line_hub,
    in_hub,
    back_border,
    ret_border,
    back_hub,
    ret_hub,
    line_back,
    line_ret,
    part,
    scattered,
    mine,
    across,
    reduced,
    landed,
    send_sem,
    recv_sem,
):
    nodes, width = feat_ref.shape
    half = width // 2
    fan = nbr_ref.shape[0]
    owners = n_group * n_member
    hub2 = 2 * hubs
    border_rows = n_member * block
    hub_base = nodes + border_rows
    g = lax.axis_index("group")
    m = lax.axis_index("member")
    hi, lo = lax.div(m, low), lax.rem(m, low)
    n_hi = n_member // low
    n_q = n_group * low
    q = g * low + lo
    piece = 2 * width // (CUTS * n_q)
    cut = n_q * piece

    loads = [
        pltpu.make_async_copy(src, dst, load_sem.at[index])
        for index, (src, dst) in enumerate(
            (
                (rows_hbm, rows_ref),
                (counts_hbm, counts_ref),
                (hubs_hbm, hubs_ref),
                (feat_hbm, feat_ref),
                (nbr_hbm, nbr_ref),
                (wself_hbm, wself_ref),
                (wnbr_hbm, wnbr_ref),
                (cot_hbm, cot_ref),
            )
        )
    ]
    for load in loads:
        load.start()

    def loop(count, body):
        lax.fori_loop(1, count, lambda step, carry: (body(step), carry)[1], 0)

    def member(step):
        down, up = n_member - step, step - 1
        down = jnp.where(down > m, down, down - 1)
        up = jnp.where(up < m, up, up + 1)
        peer = jnp.where(m < n_member // 2, down, up)
        return peer, (g, peer)

    def near(step):
        peer = lax.rem(q + step, n_q)
        return peer, (lax.div(peer, low), hi * low + lax.rem(peer, low))

    def line(step):
        peer = lax.rem(hi + step, n_hi)
        return peer, (g, peer * low + lo)

    barrier = pltpu.get_barrier_semaphore()

    def greet(device):
        pl.semaphore_signal(barrier, inc=1, device_id=device, device_id_type=MESH)

    loop(n_member, lambda step: greet(member(step)[1]))
    for step in range(1, n_group):
        for other in range(low):
            greet((lax.rem(g + step, n_group), hi * low + other))

    def copy(src, dst, which, device):
        pltpu.make_async_remote_copy(
            src_ref=src,
            dst_ref=dst,
            send_sem=send_sem.at[which],
            recv_sem=recv_sem.at[which],
            device_id=device,
            device_id_type=MESH,
        ).start()

    def rows(start, count):
        return pl.ds(pl.multiple_of(start * count, count), count)

    def to_members(src, dst, which):
        def body(step):
            peer, device = member(step)
            copy(src.at[rows(peer, block)], dst.at[rows(m, block)], which, device)

        loop(n_member, body)
        dst[rows(m, block), :] = src[rows(m, block), :]

    for load in loads[:3]:
        load.wait()
    sel_rows = select_rows(n_member, block, rows_ref[...], counts_ref[...])
    sel = jnp.concatenate([sel_rows, select_hubs(hubs, hubs_ref[...])], axis=1)
    row_of = lax.broadcasted_iota(jnp.int32, (nodes, border_rows + 128), 0)
    pick = jnp.where(row_of == sel, 1.0, 0.0).astype(BF)
    loads[3].wait()
    feat = feat_ref[...]
    picked = dot_tn(pick, feat)
    out_border[...] = picked[:border_rows].astype(BF)
    hub_wide = picked[border_rows : border_rows + hub2]
    lane_row = lax.broadcasted_iota(jnp.int32, (hub2, half), 0)
    out_hub[...] = jnp.where(lane_row < hubs, hub_wide[:, :half], hub_wide[:, half:]).astype(BF)

    pl.semaphore_wait(barrier, n_member - 1 + (n_group - 1) * low)

    loop(n_hi, lambda step: copy(out_hub, line_hub.at[hi], HUB_LINE, line(step)[1]))
    line_hub[hi] = out_hub[...]
    to_members(out_border, in_border, BORDER)

    for load in loads[4:]:
        load.wait()

    def count(names):
        names = jnp.concatenate([names] * (nodes // 128), axis=1)
        total = jnp.zeros((CHUNK, nodes), F32)
        for sample in range(fan):
            total = total + jnp.where(names == nbr_ref[sample : sample + 1, :], 1.0, 0.0)
        return total

    def chunk_names(index):
        return lax.broadcasted_iota(jnp.int32, (CHUNK, 128), 0) + index * CHUNK

    def store(index, total):
        onehot[rows(index, CHUNK), :] = total.astype(BF)
        onehot_t[:, rows(index, CHUNK)] = total.T.astype(BF)

    def fill(index, carry):
        row = chunk_names(index)
        hub_row = row - hub_base
        slab = lax.div(hub_row, hub2)
        near_id = lax.div(slab, n_hi)
        owner = (
            lax.div(near_id, low) * n_member + lax.rem(slab, n_hi) * low + lax.rem(near_id, low)
        )
        hub_name = hub_base + owner * hubs + lax.rem(hub_row, hubs)
        store(index, count(jnp.where(row < hub_base, row, hub_name)))
        return carry

    early = nodes // CHUNK
    lax.fori_loop(0, early, fill, 0)

    wait_bytes(line_hub.at[pl.ds(0, n_hi - 1)], recv_sem.at[HUB_LINE])
    loop(n_q, lambda step: copy(line_hub, in_hub.at[q], HUB_NEAR, near(step)[1]))
    in_hub[q] = line_hub[...]

    lax.fori_loop(early, onehot.shape[0] // CHUNK, fill, 0)
    pre_self = dot(feat, wself_ref[...])
    agg_sum = dot(onehot_t[:, :nodes], feat)
    feat_t = feat.astype(F32).T.astype(BF)

    wait_bytes(in_hub.at[pl.ds(0, n_q - 1)], recv_sem.at[HUB_NEAR])
    hub_half = lax.broadcasted_iota(jnp.int32, (owners * hub2, half), 0) % hub2 < hubs
    hub_rows = in_hub[...].astype(F32).reshape(owners * hub2, half)
    zero = jnp.zeros((), F32)
    hub_table = jnp.concatenate(
        [jnp.where(hub_half, hub_rows, zero), jnp.where(hub_half, zero, hub_rows)], axis=1
    ).astype(BF)
    agg_sum = agg_sum + dot(onehot_t[:, hub_base:], hub_table)
    others = (n_member - 1) * block
    wait_bytes(in_border.at[pl.ds(0, others)], recv_sem.at[BORDER])
    agg_sum = agg_sum + dot(onehot_t[:, nodes:hub_base], in_border[...])
    agg = (agg_sum * (1.0 / fan)).astype(BF)

    pre = pre_self + dot(agg, wnbr_ref[...])
    sigma = 0.5 * jnp.tanh(0.5 * pre) + 0.5
    dpre = (cot_ref[...].astype(F32) * sigma * (1.0 + pre * (1.0 - sigma))).astype(BF)

    def scatter(which):
        def body(step):
            peer, device = near(step)
            copy(
                part.at[rows(which * n_q + peer, piece)],
                scattered.at[rows(which * n_q + q, piece)],
                SCATTER + which,
                device,
            )

        loop(n_q, body)
        own = rows(which * n_q + q, piece)
        scattered[own, :] = part[own, :]

    per = width // cut
    for which in range(per):
        span = slice(which * cut, (which + 1) * cut)
        part[span, :] = dot(feat_t[span, :], dpre).astype(BF)
        scatter(which)
    dagg = dot_nt(dpre, wnbr_ref[...]) * (1.0 / fan)
    dagg = dagg.astype(BF)

    def spread(start, stop):
        return dot(onehot[start:stop, :], dagg)

    back_border[...] = spread(nodes, hub_base).astype(BF)
    to_members(back_border, ret_border, BACK_BORDER)

    agg_t = agg.astype(F32).T.astype(BF)
    for which in range(per):
        span = slice(which * cut, (which + 1) * cut)
        part[width + which * cut : width + (which + 1) * cut, :] = dot(
            agg_t[span, :], dpre
        ).astype(BF)
        scatter(per + which)

    hub_wide = spread(hub_base, hub_base + owners * hub2)
    hub_wide = jnp.where(hub_half, hub_wide[:, :half], hub_wide[:, half:])
    back_hub[...] = hub_wide.reshape(n_q, n_hi, hub2, half).astype(BF)

    def send_back(step):
        peer, device = near(step)
        copy(back_hub.at[peer], ret_hub.at[q], BACK_NEAR, device)

    loop(n_q, send_back)
    ret_hub[q] = back_hub[q]

    near_rows = (n_q - 1) * piece
    line_rows = (n_hi - 1) * piece

    def cross(which):
        wait_bytes(scattered.at[pl.ds(which * cut, near_rows)], recv_sem.at[SCATTER + which])
        summed = jnp.zeros((piece, width), F32)
        for index in range(n_q):
            start = which * cut + index * piece
            summed = summed + scattered[start : start + piece, :].astype(F32)
        source = mine.at[pl.ds(which * piece, piece)]
        source[...] = summed.astype(BF)
        slot = rows(which * n_hi + hi, piece)
        loop(n_hi, lambda step: copy(source, across.at[slot], CROSS + which, line(step)[1]))
        across[slot, :] = source[...]

    for which in range(CUTS):
        cross(which)

    total = dot_nt(dpre, wself_ref[...]) + spread(0, nodes)

    wait_bytes(ret_hub.at[pl.ds(0, n_q - 1)], recv_sem.at[BACK_NEAR])
    line_back[...] = jnp.sum(ret_hub[...].astype(F32), axis=0).astype(BF)

    def send_line(step):
        peer, device = line(step)
        copy(line_back.at[peer], line_ret.at[hi], BACK_LINE, device)

    loop(n_hi, send_line)
    line_ret[hi] = line_back[hi]

    def gather(which):
        first = which * n_hi
        wait_bytes(across.at[pl.ds(first * piece, line_rows)], recv_sem.at[CROSS + which])
        summed = lax.fori_loop(
            0,
            n_hi,
            lambda index, carry: carry + across[rows(first + index, piece), :].astype(F32),
            jnp.zeros((piece, width), F32),
            unroll=n_hi <= 16,
        )
        source = reduced.at[pl.ds(which * piece, piece)]
        source[...] = summed.astype(BF)
        slot = rows(which * n_q + q, piece)
        loop(n_q, lambda step: copy(source, landed.at[slot], GATHER + which, near(step)[1]))
        landed[slot, :] = source[...]

    for which in range(CUTS):
        gather(which)

    wait_bytes(ret_border.at[pl.ds(0, others)], recv_sem.at[BACK_BORDER])
    total = total + dot(pick[:, :border_rows], ret_border[...])
    wait_bytes(line_ret.at[pl.ds(0, n_hi - 1)], recv_sem.at[BACK_LINE])
    hub_sum = jnp.sum(line_ret[...].astype(F32), axis=0)
    top = lane_row < hubs
    hub_sum = jnp.concatenate(
        [jnp.where(top, hub_sum, zero), jnp.where(top, zero, hub_sum)], axis=1
    )
    hub_high, hub_low = split(hub_sum)
    hub_back = jnp.concatenate(
        [
            hub_high.astype(F32),
            hub_low.astype(F32),
            jnp.zeros((128 - 2 * hub2, width), F32),
        ],
        axis=0,
    ).astype(BF)
    out_ref[2 * width :, :] = 2.0 * (total + dot(pick[:, border_rows:], hub_back))

    wait_bytes(out_border.at[pl.ds(0, others)], send_sem.at[BORDER])
    wait_bytes(line_hub.at[pl.ds(0, n_hi - 1)], send_sem.at[HUB_LINE])
    wait_bytes(in_hub.at[pl.ds(0, n_q - 1)], send_sem.at[HUB_NEAR])
    wait_bytes(back_border.at[pl.ds(0, others)], send_sem.at[BACK_BORDER])
    wait_bytes(back_hub.at[pl.ds(0, n_q - 1)], send_sem.at[BACK_NEAR])
    wait_bytes(line_back.at[pl.ds(0, n_hi - 1)], send_sem.at[BACK_LINE])
    for which in range(CUTS):
        wait_bytes(part.at[pl.ds(which * cut, near_rows)], send_sem.at[SCATTER + which])
        wait_bytes(across.at[pl.ds(which * n_hi * piece, line_rows)], send_sem.at[CROSS + which])
    for which in range(CUTS):
        wait_bytes(landed.at[pl.ds(which * cut, near_rows)], recv_sem.at[GATHER + which])
        span = slice(which * cut, (which + 1) * cut)
        out_ref[span, :] = landed[span, :].astype(F32)
        wait_bytes(part.at[pl.ds(which * cut, near_rows)], send_sem.at[GATHER + which])


def local(features, neighbours, send_rows, block_counts, hub_rows, w_self, w_nbr, cotangent):
    nodes, width = features.shape
    n_member = lax.axis_size("member")
    n_group = lax.axis_size("group")
    block = send_rows.shape[1]
    hubs = hub_rows.shape[1]
    owners = n_group * n_member
    hub2 = 2 * hubs
    low = max(1, 8 // n_group)
    n_q = n_group * low
    n_hi = n_member // low
    piece = 2 * width // (CUTS * n_q)
    half = width // 2
    border_rows = n_member * block
    table_rows = nodes + border_rows + owners * hub2
    border = pltpu.VMEM((border_rows, width), BF)
    hub_line = pltpu.VMEM((n_hi, hub2, half), BF)
    hub_all = pltpu.VMEM((n_q, n_hi, hub2, half), BF)
    pair = pltpu.VMEM((2 * width, width), BF)
    result = pl.pallas_call(
        functools.partial(kernel, n_group, n_member, low, block, hubs),
        out_shape=pltpu.VMEM((2 * width + nodes, width), F32),
        in_specs=[pl.BlockSpec(memory_space=pltpu.HBM)] * 8,
        out_specs=pl.BlockSpec(memory_space=pltpu.VMEM),
        scratch_shapes=[
            pltpu.VMEM((nodes, width), BF),
            pltpu.VMEM((neighbours.shape[1], nodes), jnp.int32),
            pltpu.VMEM(send_rows.shape, jnp.int32),
            pltpu.VMEM((1, n_member), jnp.int32),
            pltpu.VMEM(hub_rows.shape, jnp.int32),
            pltpu.VMEM((width, width), BF),
            pltpu.VMEM((width, width), BF),
            pltpu.VMEM((nodes, width), BF),
            pltpu.SemaphoreType.DMA((8,)),
            pltpu.VMEM((table_rows, nodes), BF),
            pltpu.VMEM((nodes, table_rows), BF),
            border,
            border,
            pltpu.VMEM((hub2, half), BF),
            hub_line,
            hub_all,
            border,
            border,
            hub_all,
            hub_all,
            hub_line,
            hub_line,
            pair,
            pair,
            pltpu.VMEM((CUTS * piece, width), BF),
            pltpu.VMEM((CUTS * n_hi * piece, width), BF),
            pltpu.VMEM((CUTS * piece, width), BF),
            pair,
            pltpu.SemaphoreType.DMA((SEMS,)),
            pltpu.SemaphoreType.DMA((SEMS,)),
        ],
        compiler_params=pltpu.CompilerParams(
            collective_id=0, has_side_effects=True, vmem_limit_bytes=60 * 1024 * 1024
        ),
    )(
        features,
        neighbours.T,
        send_rows,
        block_counts.reshape(1, -1),
        hub_rows,
        w_self,
        w_nbr,
        cotangent,
    )
    scale = 1.0 / math.sqrt(nodes * owners)
    grad_self = result[:width] * scale
    grad_nbr = result[width : 2 * width] * scale
    return (grad_self, grad_nbr, (0.5 * result[2 * width :]).astype(BF))


def solution(mesh):
    in_specs = (
        P(("group", "member"), None),
        P(("group", "member"), None),
        P(("group", "member"), None),
        P(("group", "member")),
        P(("group", "member"), None),
        P(),
        P(),
        P(("group", "member"), None),
    )
    out_specs = (P(), P(), P(("group", "member"), None))
    return jax.shard_map(local, mesh=mesh, in_specs=in_specs, out_specs=out_specs, check_vma=False)
```

```python
import functools
import math

import jax
import jax.numpy as jnp
from jax import lax
from jax.experimental import pallas as pl
from jax.experimental.pallas import tpu as pltpu
from jax.sharding import PartitionSpec as P

MESH = pl.DeviceIdType.MESH
BF = jnp.bfloat16
F32 = jnp.float32
CHUNK = 128
BORDER, HUB_LINE, HUB_NEAR, BACK_BORDER, BACK_NEAR, BACK_LINE = range(6)
SCATTER, CROSS, GATHER = 6, 8, 10
SEMS = 12


def dot(a, b):
    return jnp.dot(a, b, preferred_element_type=F32)


def dot_tn(a, b):
    return lax.dot_general(a, b, (((0,), (0,)), ((), ())), preferred_element_type=F32)


def dot_nt(a, b):
    return lax.dot_general(a, b, (((1,), (1,)), ((), ())), preferred_element_type=F32)


def split(value):
    high = value.astype(BF)
    return high, (value - high.astype(F32)).astype(BF)


def wait_bytes(ref, sem):
    pltpu.make_async_copy(ref, ref, sem).wait()


def select_rows(n_member, block, send_rows, counts):
    lanes = n_member * block
    lane = lax.broadcasted_iota(jnp.int32, (n_member, lanes), 1)
    peer = lax.broadcasted_iota(jnp.int32, (n_member, lanes), 0)
    own = lane // block == peer
    slot = lax.broadcasted_iota(jnp.int32, (block, lanes), 0)
    slot_lane = lax.broadcasted_iota(jnp.int32, (block, lanes), 1) % block
    expand = jnp.where(slot == slot_lane, 1.0, 0.0).astype(BF)
    spread_rows = dot(send_rows.astype(F32).astype(BF), expand)
    row = jnp.sum(jnp.where(own, spread_rows, 0.0), axis=0, keepdims=True)
    repeat = jnp.where(own, 1.0, 0.0).astype(BF)
    counts = jnp.broadcast_to(counts.astype(F32), (8, n_member)).astype(BF)
    live = dot(counts, repeat)[:1].astype(jnp.int32)
    lane = lax.broadcasted_iota(jnp.int32, (1, lanes), 1)
    return jnp.where(lane % block < live, row.astype(jnp.int32), -1)


def select_hubs(hubs, hub_rows):
    lane = lax.broadcasted_iota(jnp.int32, (hubs, 128), 1)
    hub = lax.broadcasted_iota(jnp.int32, (hubs, 128), 0)
    repeat = jnp.where(lane % hubs == hub, 1.0, 0.0).astype(BF)
    wide = jnp.broadcast_to(hub_rows.astype(F32), (8, hubs)).astype(BF)
    row = dot(wide, repeat)[:1].astype(jnp.int32)
    lane = lax.broadcasted_iota(jnp.int32, (1, 128), 1)
    return jnp.where(lane < 4 * hubs, row, -1)


def kernel(
    n_group,
    n_member,
    low,
    cuts,
    block,
    hubs,
    feat_hbm,
    nbr_hbm,
    rows_hbm,
    counts_hbm,
    hubs_hbm,
    wself_hbm,
    wnbr_hbm,
    cot_hbm,
    out_ref,
    feat_ref,
    nbr_ref,
    rows_ref,
    counts_ref,
    hubs_ref,
    wself_ref,
    wnbr_ref,
    cot_ref,
    load_sem,
    onehot,
    onehot_t,
    out_border,
    in_border,
    out_hub,
    line_hub,
    in_hub,
    back_border,
    ret_border,
    back_hub,
    ret_hub,
    line_back,
    line_ret,
    part,
    scattered,
    mine,
    across,
    reduced,
    landed,
    send_sem,
    recv_sem,
):
    nodes, width = feat_ref.shape
    half = width // 2
    fan = nbr_ref.shape[0]
    owners = n_group * n_member
    hub2 = 2 * hubs
    border_rows = n_member * block
    hub_base = nodes + border_rows
    g = lax.axis_index("group")
    m = lax.axis_index("member")
    hi, lo = lax.div(m, low), lax.rem(m, low)
    n_hi = n_member // low
    n_q = n_group * low
    q = g * low + lo
    piece = 2 * width // (cuts * n_q)
    cut = n_q * piece

    loads = [
        pltpu.make_async_copy(src, dst, load_sem.at[index])
        for index, (src, dst) in enumerate(
            (
                (rows_hbm, rows_ref),
                (counts_hbm, counts_ref),
                (hubs_hbm, hubs_ref),
                (feat_hbm, feat_ref),
                (nbr_hbm, nbr_ref),
                (wself_hbm, wself_ref),
                (wnbr_hbm, wnbr_ref),
                (cot_hbm, cot_ref),
            )
        )
    ]
    for load in loads:
        load.start()

    def loop(count, body):
        lax.fori_loop(1, count, lambda step, carry: (body(step), carry)[1], 0)

    def member(step):
        down, up = n_member - step, step - 1
        down = jnp.where(down > m, down, down - 1)
        up = jnp.where(up < m, up, up + 1)
        peer = jnp.where(m < n_member // 2, down, up)
        return peer, (g, peer)

    def near(step):
        peer = lax.rem(q + step, n_q)
        return peer, (lax.div(peer, low), hi * low + lax.rem(peer, low))

    def line(step):
        peer = lax.rem(hi + step, n_hi)
        return peer, (g, peer * low + lo)

    barrier = pltpu.get_barrier_semaphore()

    def greet(device):
        pl.semaphore_signal(barrier, inc=1, device_id=device, device_id_type=MESH)

    loop(n_member, lambda step: greet(member(step)[1]))
    for step in range(1, n_group):
        for other in range(low):
            greet((lax.rem(g + step, n_group), hi * low + other))

    def copy(src, dst, which, device):
        pltpu.make_async_remote_copy(
            src_ref=src,
            dst_ref=dst,
            send_sem=send_sem.at[which],
            recv_sem=recv_sem.at[which],
            device_id=device,
            device_id_type=MESH,
        ).start()

    def rows(start, count):
        return pl.ds(pl.multiple_of(start * count, count), count)

    def to_members(src, dst, which):
        def body(step):
            peer, device = member(step)
            copy(src.at[rows(peer, block)], dst.at[rows(m, block)], which, device)

        loop(n_member, body)
        dst[rows(m, block), :] = src[rows(m, block), :]

    for load in loads[:3]:
        load.wait()
    sel_rows = select_rows(n_member, block, rows_ref[...], counts_ref[...])
    sel = jnp.concatenate([sel_rows, select_hubs(hubs, hubs_ref[...])], axis=1)
    row_of = lax.broadcasted_iota(jnp.int32, (nodes, border_rows + 128), 0)
    pick = jnp.where(row_of == sel, 1.0, 0.0).astype(BF)
    loads[3].wait()
    feat = feat_ref[...]
    picked = dot_tn(pick, feat)
    out_border[...] = picked[:border_rows].astype(BF)
    hub_wide = picked[border_rows : border_rows + hub2]
    lane_row = lax.broadcasted_iota(jnp.int32, (hub2, half), 0)
    out_hub[...] = jnp.where(lane_row < hubs, hub_wide[:, :half], hub_wide[:, half:]).astype(BF)

    pl.semaphore_wait(barrier, n_member - 1 + (n_group - 1) * low)

    loop(n_hi, lambda step: copy(out_hub, line_hub.at[hi], HUB_LINE, line(step)[1]))
    line_hub[hi] = out_hub[...]
    to_members(out_border, in_border, BORDER)

    for load in loads[4:]:
        load.wait()

    def count(names):
        names = jnp.concatenate([names] * (nodes // 128), axis=1)
        total = jnp.zeros((CHUNK, nodes), F32)
        for sample in range(fan):
            total = total + jnp.where(names == nbr_ref[sample : sample + 1, :], 1.0, 0.0)
        return total

    def chunk_names(index):
        return lax.broadcasted_iota(jnp.int32, (CHUNK, 128), 0) + index * CHUNK

    def store(index, total):
        onehot[rows(index, CHUNK), :] = total.astype(BF)
        onehot_t[:, rows(index, CHUNK)] = total.T.astype(BF)

    def fill(index, carry):
        row = chunk_names(index)
        hub_row = row - hub_base
        slab = lax.div(hub_row, hub2)
        near_id = lax.div(slab, n_hi)
        owner = (
            lax.div(near_id, low) * n_member + lax.rem(slab, n_hi) * low + lax.rem(near_id, low)
        )
        hub_name = hub_base + owner * hubs + lax.rem(hub_row, hubs)
        store(index, count(jnp.where(row < hub_base, row, hub_name)))
        return carry

    early = nodes // CHUNK
    lax.fori_loop(0, early, fill, 0)

    if n_hi > 1:
        wait_bytes(line_hub.at[pl.ds(0, n_hi - 1)], recv_sem.at[HUB_LINE])
    loop(n_q, lambda step: copy(line_hub, in_hub.at[q], HUB_NEAR, near(step)[1]))
    in_hub[q] = line_hub[...]

    lax.fori_loop(early, onehot.shape[0] // CHUNK, fill, 0)
    pre_self = dot(feat, wself_ref[...])
    agg_sum = dot(onehot_t[:, :nodes], feat)
    feat_t = feat.astype(F32).T.astype(BF)

    wait_bytes(in_hub.at[pl.ds(0, n_q - 1)], recv_sem.at[HUB_NEAR])
    hub_half = lax.broadcasted_iota(jnp.int32, (owners * hub2, half), 0) % hub2 < hubs
    hub_rows = in_hub[...].astype(F32).reshape(owners * hub2, half)
    zero = jnp.zeros((), F32)
    hub_table = jnp.concatenate(
        [jnp.where(hub_half, hub_rows, zero), jnp.where(hub_half, zero, hub_rows)], axis=1
    ).astype(BF)
    agg_sum = agg_sum + dot(onehot_t[:, hub_base:], hub_table)
    others = (n_member - 1) * block
    wait_bytes(in_border.at[pl.ds(0, others)], recv_sem.at[BORDER])
    agg_sum = agg_sum + dot(onehot_t[:, nodes:hub_base], in_border[...])
    agg = (agg_sum * (1.0 / fan)).astype(BF)

    pre = pre_self + dot(agg, wnbr_ref[...])
    sigma = 0.5 * jnp.tanh(0.5 * pre) + 0.5
    dpre = (cot_ref[...].astype(F32) * sigma * (1.0 + pre * (1.0 - sigma))).astype(BF)

    def scatter(which):
        def body(step):
            peer, device = near(step)
            copy(
                part.at[rows(which * n_q + peer, piece)],
                scattered.at[rows(which * n_q + q, piece)],
                SCATTER + which,
                device,
            )

        loop(n_q, body)
        own = rows(which * n_q + q, piece)
        scattered[own, :] = part[own, :]

    part[:width, :] = dot(feat_t, dpre).astype(BF)
    if cuts == 2:
        scatter(0)
    part[width:, :] = dot_tn(agg, dpre).astype(BF)
    scatter(cuts - 1)

    dagg = dot_nt(dpre, wnbr_ref[...]) * (1.0 / fan)
    dagg = dagg.astype(BF)

    def spread(start, stop):
        return dot(onehot[start:stop, :], dagg)

    hub_wide = spread(hub_base, hub_base + owners * hub2)
    hub_wide = jnp.where(hub_half, hub_wide[:, :half], hub_wide[:, half:])
    back_hub[...] = hub_wide.reshape(n_q, n_hi, hub2, half).astype(BF)

    def send_back(step):
        peer, device = near(step)
        copy(back_hub.at[peer], ret_hub.at[q], BACK_NEAR, device)

    loop(n_q, send_back)
    ret_hub[q] = back_hub[q]
    back_border[...] = spread(nodes, hub_base).astype(BF)
    to_members(back_border, ret_border, BACK_BORDER)

    near_rows = (n_q - 1) * piece
    line_rows = (n_hi - 1) * piece

    def cross(which):
        wait_bytes(scattered.at[pl.ds(which * cut, near_rows)], recv_sem.at[SCATTER + which])
        summed = jnp.zeros((piece, width), F32)
        for index in range(n_q):
            start = which * cut + index * piece
            summed = summed + scattered[start : start + piece, :].astype(F32)
        source = mine.at[pl.ds(which * piece, piece)]
        source[...] = summed.astype(BF)
        slot = rows(which * n_hi + hi, piece)
        loop(n_hi, lambda step: copy(source, across.at[slot], CROSS + which, line(step)[1]))
        across[slot, :] = source[...]

    for which in range(cuts):
        cross(which)

    total = dot_nt(dpre, wself_ref[...]) + spread(0, nodes)

    wait_bytes(ret_hub.at[pl.ds(0, n_q - 1)], recv_sem.at[BACK_NEAR])
    line_back[...] = jnp.sum(ret_hub[...].astype(F32), axis=0).astype(BF)

    def send_line(step):
        peer, device = line(step)
        copy(line_back.at[peer], line_ret.at[hi], BACK_LINE, device)

    loop(n_hi, send_line)
    line_ret[hi] = line_back[hi]

    def gather(which):
        first = which * n_hi
        if n_hi > 1:
            wait_bytes(across.at[pl.ds(first * piece, line_rows)], recv_sem.at[CROSS + which])
        summed = lax.fori_loop(
            0,
            n_hi,
            lambda index, carry: carry + across[rows(first + index, piece), :].astype(F32),
            jnp.zeros((piece, width), F32),
            unroll=n_hi <= 16,
        )
        source = reduced.at[pl.ds(which * piece, piece)]
        source[...] = summed.astype(BF)
        slot = rows(which * n_q + q, piece)
        loop(n_q, lambda step: copy(source, landed.at[slot], GATHER + which, near(step)[1]))
        landed[slot, :] = source[...]

    for which in range(cuts):
        gather(which)

    wait_bytes(ret_border.at[pl.ds(0, others)], recv_sem.at[BACK_BORDER])
    total = total + dot(pick[:, :border_rows], ret_border[...])
    if n_hi > 1:
        wait_bytes(line_ret.at[pl.ds(0, n_hi - 1)], recv_sem.at[BACK_LINE])
    hub_sum = jnp.sum(line_ret[...].astype(F32), axis=0)
    top = lane_row < hubs
    hub_sum = jnp.concatenate(
        [jnp.where(top, hub_sum, zero), jnp.where(top, zero, hub_sum)], axis=1
    )
    hub_high, hub_low = split(hub_sum)
    hub_back = jnp.concatenate(
        [
            hub_high.astype(F32),
            hub_low.astype(F32),
            jnp.zeros((128 - 2 * hub2, width), F32),
        ],
        axis=0,
    ).astype(BF)
    out_ref[2 * width :, :] = 2.0 * (total + dot(pick[:, border_rows:], hub_back))

    wait_bytes(out_border.at[pl.ds(0, others)], send_sem.at[BORDER])
    if n_hi > 1:
        wait_bytes(line_hub.at[pl.ds(0, n_hi - 1)], send_sem.at[HUB_LINE])
    wait_bytes(in_hub.at[pl.ds(0, n_q - 1)], send_sem.at[HUB_NEAR])
    wait_bytes(back_border.at[pl.ds(0, others)], send_sem.at[BACK_BORDER])
    wait_bytes(back_hub.at[pl.ds(0, n_q - 1)], send_sem.at[BACK_NEAR])
    if n_hi > 1:
        wait_bytes(line_back.at[pl.ds(0, n_hi - 1)], send_sem.at[BACK_LINE])
    for which in range(cuts):
        wait_bytes(part.at[pl.ds(which * cut, near_rows)], send_sem.at[SCATTER + which])
        if n_hi > 1:
            wait_bytes(
                across.at[pl.ds(which * n_hi * piece, line_rows)], send_sem.at[CROSS + which]
            )
    for which in range(cuts):
        wait_bytes(landed.at[pl.ds(which * cut, near_rows)], recv_sem.at[GATHER + which])
        span = slice(which * cut, (which + 1) * cut)
        out_ref[span, :] = landed[span, :].astype(F32)
        wait_bytes(part.at[pl.ds(which * cut, near_rows)], send_sem.at[GATHER + which])


def local(features, neighbours, send_rows, block_counts, hub_rows, w_self, w_nbr, cotangent):
    nodes, width = features.shape
    n_member = lax.axis_size("member")
    n_group = lax.axis_size("group")
    block = send_rows.shape[1]
    hubs = hub_rows.shape[1]
    owners = n_group * n_member
    hub2 = 2 * hubs
    low, cuts = max(1, 8 // n_group), 2
    if 2 * width % (16 * owners) == 0:
        low, cuts = n_member, 1
    n_q = n_group * low
    n_hi = n_member // low
    piece = 2 * width // (cuts * n_q)
    half = width // 2
    border_rows = n_member * block
    table_rows = nodes + border_rows + owners * hub2
    border = pltpu.VMEM((border_rows, width), BF)
    hub_line = pltpu.VMEM((n_hi, hub2, half), BF)
    hub_all = pltpu.VMEM((n_q, n_hi, hub2, half), BF)
    pair = pltpu.VMEM((2 * width, width), BF)
    result = pl.pallas_call(
        functools.partial(kernel, n_group, n_member, low, cuts, block, hubs),
        out_shape=pltpu.VMEM((2 * width + nodes, width), F32),
        in_specs=[pl.BlockSpec(memory_space=pltpu.HBM)] * 8,
        out_specs=pl.BlockSpec(memory_space=pltpu.VMEM),
        scratch_shapes=[
            pltpu.VMEM((nodes, width), BF),
            pltpu.VMEM((neighbours.shape[1], nodes), jnp.int32),
            pltpu.VMEM(send_rows.shape, jnp.int32),
            pltpu.VMEM((1, n_member), jnp.int32),
            pltpu.VMEM(hub_rows.shape, jnp.int32),
            pltpu.VMEM((width, width), BF),
            pltpu.VMEM((width, width), BF),
            pltpu.VMEM((nodes, width), BF),
            pltpu.SemaphoreType.DMA((8,)),
            pltpu.VMEM((table_rows, nodes), BF),
            pltpu.VMEM((nodes, table_rows), BF),
            border,
            border,
            pltpu.VMEM((hub2, half), BF),
            hub_line,
            hub_all,
            border,
            border,
            hub_all,
            hub_all,
            hub_line,
            hub_line,
            pair,
            pair,
            pltpu.VMEM((cuts * piece, width), BF),
            pltpu.VMEM((cuts * n_hi * piece, width), BF),
            pltpu.VMEM((cuts * piece, width), BF),
            pair,
            pltpu.SemaphoreType.DMA((SEMS,)),
            pltpu.SemaphoreType.DMA((SEMS,)),
        ],
        compiler_params=pltpu.CompilerParams(
            collective_id=0, has_side_effects=True, vmem_limit_bytes=60 * 1024 * 1024
        ),
    )(
        features,
        neighbours.T,
        send_rows,
        block_counts.reshape(1, -1),
        hub_rows,
        w_self,
        w_nbr,
        cotangent,
    )
    scale = 1.0 / math.sqrt(nodes * owners)
    grad_self = result[:width] * scale
    grad_nbr = result[width : 2 * width] * scale
    return (grad_self, grad_nbr, (0.5 * result[2 * width :]).astype(BF))


def solution(mesh):
    in_specs = (
        P(("group", "member"), None),
        P(("group", "member"), None),
        P(("group", "member"), None),
        P(("group", "member")),
        P(("group", "member"), None),
        P(),
        P(),
        P(("group", "member"), None),
    )
    out_specs = (P(), P(), P(("group", "member"), None))
    return jax.shard_map(local, mesh=mesh, in_specs=in_specs, out_specs=out_specs, check_vma=False)
```

```python
import functools
import math

import jax
import jax.numpy as jnp
from jax import lax
from jax.experimental import pallas as pl
from jax.experimental.pallas import tpu as pltpu
from jax.sharding import PartitionSpec as P

MESH = pl.DeviceIdType.MESH
BF = jnp.bfloat16
F32 = jnp.float32
CHUNK = 128
CUTS = 2
BORDER, HUB_LINE, HUB_NEAR, BACK_BORDER, BACK_NEAR, BACK_LINE = range(6)
SCATTER, CROSS, GATHER = 6, 6 + CUTS, 6 + 2 * CUTS
SEMS = 6 + 3 * CUTS


def dot(a, b):
    return jnp.dot(a, b, preferred_element_type=F32)


def dot_tn(a, b):
    return lax.dot_general(a, b, (((0,), (0,)), ((), ())), preferred_element_type=F32)


def dot_nt(a, b):
    return lax.dot_general(a, b, (((1,), (1,)), ((), ())), preferred_element_type=F32)


def split(value):
    high = value.astype(BF)
    return high, (value - high.astype(F32)).astype(BF)


def wait_bytes(ref, sem):
    pltpu.make_async_copy(ref, ref, sem).wait()


def select_rows(n_member, block, send_rows, counts):
    lanes = n_member * block
    lane = lax.broadcasted_iota(jnp.int32, (n_member, lanes), 1)
    peer = lax.broadcasted_iota(jnp.int32, (n_member, lanes), 0)
    own = lane // block == peer
    slot = lax.broadcasted_iota(jnp.int32, (block, lanes), 0)
    slot_lane = lax.broadcasted_iota(jnp.int32, (block, lanes), 1) % block
    expand = jnp.where(slot == slot_lane, 1.0, 0.0).astype(BF)
    spread_rows = dot(send_rows.astype(F32).astype(BF), expand)
    row = jnp.sum(jnp.where(own, spread_rows, 0.0), axis=0, keepdims=True)
    repeat = jnp.where(own, 1.0, 0.0).astype(BF)
    counts = jnp.broadcast_to(counts.astype(F32), (8, n_member)).astype(BF)
    live = dot(counts, repeat)[:1].astype(jnp.int32)
    lane = lax.broadcasted_iota(jnp.int32, (1, lanes), 1)
    return jnp.where(lane % block < live, row.astype(jnp.int32), -1)


def select_hubs(hubs, hub_rows):
    lane = lax.broadcasted_iota(jnp.int32, (hubs, 128), 1)
    hub = lax.broadcasted_iota(jnp.int32, (hubs, 128), 0)
    repeat = jnp.where(lane % hubs == hub, 1.0, 0.0).astype(BF)
    wide = jnp.broadcast_to(hub_rows.astype(F32), (8, hubs)).astype(BF)
    row = dot(wide, repeat)[:1].astype(jnp.int32)
    lane = lax.broadcasted_iota(jnp.int32, (1, 128), 1)
    return jnp.where(lane < 4 * hubs, row, -1)


def kernel(
    n_group,
    n_member,
    low,
    block,
    hubs,
    feat_hbm,
    nbr_hbm,
    rows_hbm,
    counts_hbm,
    hubs_hbm,
    wself_hbm,
    wnbr_hbm,
    cot_hbm,
    out_ref,
    feat_ref,
    nbr_ref,
    rows_ref,
    counts_ref,
    hubs_ref,
    wself_ref,
    wnbr_ref,
    cot_ref,
    load_sem,
    onehot,
    onehot_t,
    out_border,
    in_border,
    out_hub,
    line_hub,
    in_hub,
    back_border,
    ret_border,
    back_hub,
    ret_hub,
    line_back,
    line_ret,
    part,
    scattered,
    mine,
    across,
    reduced,
    send_sem,
    recv_sem,
):
    nodes, width = feat_ref.shape
    half = width // 2
    fan = nbr_ref.shape[0]
    owners = n_group * n_member
    hub2 = 2 * hubs
    border_rows = n_member * block
    hub_base = nodes + border_rows
    g = lax.axis_index("group")
    m = lax.axis_index("member")
    hi, lo = lax.div(m, low), lax.rem(m, low)
    n_hi = n_member // low
    n_q = n_group * low
    q = g * low + lo
    piece = 2 * width // (CUTS * n_q)
    cut = n_q * piece

    loads = [
        pltpu.make_async_copy(src, dst, load_sem.at[index])
        for index, (src, dst) in enumerate(
            (
                (rows_hbm, rows_ref),
                (counts_hbm, counts_ref),
                (hubs_hbm, hubs_ref),
                (feat_hbm, feat_ref),
                (nbr_hbm, nbr_ref),
                (wself_hbm, wself_ref),
                (wnbr_hbm, wnbr_ref),
                (cot_hbm, cot_ref),
            )
        )
    ]
    for load in loads:
        load.start()

    def loop(count, body):
        lax.fori_loop(1, count, lambda step, carry: (body(step), carry)[1], 0)

    def member(step):
        down, up = n_member - step, step - 1
        down = jnp.where(down > m, down, down - 1)
        up = jnp.where(up < m, up, up + 1)
        peer = jnp.where(m < n_member // 2, down, up)
        return peer, (g, peer)

    def near(step):
        peer = lax.rem(q + step, n_q)
        return peer, (lax.div(peer, low), hi * low + lax.rem(peer, low))

    def line(step):
        peer = lax.rem(hi + step, n_hi)
        return peer, (g, peer * low + lo)

    barrier = pltpu.get_barrier_semaphore()

    def greet(device):
        pl.semaphore_signal(barrier, inc=1, device_id=device, device_id_type=MESH)

    loop(n_member, lambda step: greet(member(step)[1]))
    for step in range(1, n_group):
        for other in range(low):
            greet((lax.rem(g + step, n_group), hi * low + other))

    def copy(src, dst, which, device):
        pltpu.make_async_remote_copy(
            src_ref=src,
            dst_ref=dst,
            send_sem=send_sem.at[which],
            recv_sem=recv_sem.at[which],
            device_id=device,
            device_id_type=MESH,
        ).start()

    def rows(start, count):
        return pl.ds(pl.multiple_of(start * count, count), count)

    def to_members(src, dst, which):
        def body(step):
            peer, device = member(step)
            copy(src.at[rows(peer, block)], dst.at[rows(m, block)], which, device)

        loop(n_member, body)
        dst[rows(m, block), :] = src[rows(m, block), :]

    for load in loads[:3]:
        load.wait()
    sel_rows = select_rows(n_member, block, rows_ref[...], counts_ref[...])
    sel = jnp.concatenate([sel_rows, select_hubs(hubs, hubs_ref[...])], axis=1)
    row_of = lax.broadcasted_iota(jnp.int32, (nodes, border_rows + 128), 0)
    pick = jnp.where(row_of == sel, 1.0, 0.0).astype(BF)
    loads[3].wait()
    feat = feat_ref[...]
    picked = dot_tn(pick, feat)
    out_border[...] = picked[:border_rows].astype(BF)
    hub_wide = picked[border_rows : border_rows + hub2]
    lane_row = lax.broadcasted_iota(jnp.int32, (hub2, half), 0)
    out_hub[...] = jnp.where(lane_row < hubs, hub_wide[:, :half], hub_wide[:, half:]).astype(BF)

    pl.semaphore_wait(barrier, n_member - 1 + (n_group - 1) * low)

    loop(n_hi, lambda step: copy(out_hub, line_hub.at[hi], HUB_LINE, line(step)[1]))
    line_hub[hi] = out_hub[...]
    to_members(out_border, in_border, BORDER)

    for load in loads[4:]:
        load.wait()

    def count(names):
        names = jnp.concatenate([names] * (nodes // 128), axis=1)
        total = jnp.zeros((CHUNK, nodes), F32)
        for sample in range(fan):
            total = total + jnp.where(names == nbr_ref[sample : sample + 1, :], 1.0, 0.0)
        return total

    def chunk_names(index):
        return lax.broadcasted_iota(jnp.int32, (CHUNK, 128), 0) + index * CHUNK

    def store(index, total):
        onehot[rows(index, CHUNK), :] = total.astype(BF)
        onehot_t[:, rows(index, CHUNK)] = total.T.astype(BF)

    def fill(index, carry):
        row = chunk_names(index)
        hub_row = row - hub_base
        slab = lax.div(hub_row, hub2)
        near_id = lax.div(slab, n_hi)
        owner = (
            lax.div(near_id, low) * n_member + lax.rem(slab, n_hi) * low + lax.rem(near_id, low)
        )
        hub_name = hub_base + owner * hubs + lax.rem(hub_row, hubs)
        store(index, count(jnp.where(row < hub_base, row, hub_name)))
        return carry

    early = nodes // CHUNK
    lax.fori_loop(0, early, fill, 0)

    wait_bytes(line_hub.at[pl.ds(0, n_hi - 1)], recv_sem.at[HUB_LINE])
    loop(n_q, lambda step: copy(line_hub, in_hub.at[q], HUB_NEAR, near(step)[1]))
    in_hub[q] = line_hub[...]

    lax.fori_loop(early, onehot.shape[0] // CHUNK, fill, 0)
    pre_self = dot(feat, wself_ref[...])
    agg_sum = dot(onehot_t[:, :nodes], feat)
    feat_t = feat.astype(F32).T.astype(BF)

    wait_bytes(in_hub.at[pl.ds(0, n_q - 1)], recv_sem.at[HUB_NEAR])
    hub_half = lax.broadcasted_iota(jnp.int32, (owners * hub2, half), 0) % hub2 < hubs
    hub_rows = in_hub[...].astype(F32).reshape(owners * hub2, half)
    zero = jnp.zeros((), F32)
    hub_table = jnp.concatenate(
        [jnp.where(hub_half, hub_rows, zero), jnp.where(hub_half, zero, hub_rows)], axis=1
    ).astype(BF)
    agg_sum = agg_sum + dot(onehot_t[:, hub_base:], hub_table)
    others = (n_member - 1) * block
    wait_bytes(in_border.at[pl.ds(0, others)], recv_sem.at[BORDER])
    agg_sum = agg_sum + dot(onehot_t[:, nodes:hub_base], in_border[...])
    agg = (agg_sum * (1.0 / fan)).astype(BF)

    pre = pre_self + dot(agg, wnbr_ref[...])
    sigma = 0.5 * jnp.tanh(0.5 * pre) + 0.5
    dpre = (cot_ref[...].astype(F32) * sigma * (1.0 + pre * (1.0 - sigma))).astype(BF)

    def scatter(which):
        def body(step):
            peer, device = near(step)
            copy(
                part.at[rows(which * n_q + peer, piece)],
                scattered.at[rows(which * n_q + q, piece)],
                SCATTER + which,
                device,
            )

        loop(n_q, body)
        own = rows(which * n_q + q, piece)
        scattered[own, :] = part[own, :]

    per = width // cut
    for which in range(per):
        span = slice(which * cut, (which + 1) * cut)
        part[span, :] = dot(feat_t[span, :], dpre).astype(BF)
        scatter(which)
    agg_t = agg.astype(F32).T.astype(BF)
    for which in range(per):
        span = slice(which * cut, (which + 1) * cut)
        part[width + which * cut : width + (which + 1) * cut, :] = dot(
            agg_t[span, :], dpre
        ).astype(BF)
        scatter(per + which)

    dagg = dot_nt(dpre, wnbr_ref[...]) * (1.0 / fan)
    dagg = dagg.astype(BF)

    def spread(start, stop):
        return dot(onehot[start:stop, :], dagg)

    hub_wide = spread(hub_base, hub_base + owners * hub2)
    hub_wide = jnp.where(hub_half, hub_wide[:, :half], hub_wide[:, half:])
    back_hub[...] = hub_wide.reshape(n_q, n_hi, hub2, half).astype(BF)

    def send_back(step):
        peer, device = near(step)
        copy(back_hub.at[peer], ret_hub.at[q], BACK_NEAR, device)

    loop(n_q, send_back)
    ret_hub[q] = back_hub[q]
    back_border[...] = spread(nodes, hub_base).astype(BF)
    to_members(back_border, ret_border, BACK_BORDER)

    near_rows = (n_q - 1) * piece
    line_rows = (n_hi - 1) * piece

    def cross(which):
        wait_bytes(scattered.at[pl.ds(which * cut, near_rows)], recv_sem.at[SCATTER + which])
        summed = jnp.zeros((piece, width), F32)
        for index in range(n_q):
            start = which * cut + index * piece
            summed = summed + scattered[start : start + piece, :].astype(F32)
        source = mine.at[pl.ds(which * piece, piece)]
        source[...] = summed.astype(BF)
        slot = rows(which * n_hi + hi, piece)
        loop(n_hi, lambda step: copy(source, across.at[slot], CROSS + which, line(step)[1]))
        across[slot, :] = source[...]

    for which in range(CUTS):
        cross(which)

    total = dot_nt(dpre, wself_ref[...]) + spread(0, nodes)

    wait_bytes(ret_hub.at[pl.ds(0, n_q - 1)], recv_sem.at[BACK_NEAR])
    line_back[...] = jnp.sum(ret_hub[...].astype(F32), axis=0).astype(BF)

    def send_line(step):
        peer, device = line(step)
        copy(line_back.at[peer], line_ret.at[hi], BACK_LINE, device)

    loop(n_hi, send_line)
    line_ret[hi] = line_back[hi]

    def gather(which):
        first = which * n_hi
        wait_bytes(across.at[pl.ds(first * piece, line_rows)], recv_sem.at[CROSS + which])
        summed = lax.fori_loop(
            0,
            n_hi,
            lambda index, carry: carry + across[rows(first + index, piece), :].astype(F32),
            jnp.zeros((piece, width), F32),
            unroll=n_hi <= 16,
        )
        source = reduced.at[pl.ds(which * piece, piece)]
        source[...] = summed.astype(BF)
        slot = rows(which * n_q + q, piece)
        loop(n_q, lambda step: copy(source, out_ref.at[slot], GATHER + which, near(step)[1]))
        out_ref[slot, :] = source[...]

    for which in range(CUTS):
        gather(which)

    wait_bytes(ret_border.at[pl.ds(0, others)], recv_sem.at[BACK_BORDER])
    total = total + dot(pick[:, :border_rows], ret_border[...])
    wait_bytes(line_ret.at[pl.ds(0, n_hi - 1)], recv_sem.at[BACK_LINE])
    hub_sum = jnp.sum(line_ret[...].astype(F32), axis=0)
    top = lane_row < hubs
    hub_sum = jnp.concatenate(
        [jnp.where(top, hub_sum, zero), jnp.where(top, zero, hub_sum)], axis=1
    )
    hub_high, hub_low = split(hub_sum)
    hub_back = jnp.concatenate(
        [
            hub_high.astype(F32),
            hub_low.astype(F32),
            jnp.zeros((128 - 2 * hub2, width), F32),
        ],
        axis=0,
    ).astype(BF)
    out_ref[2 * width :, :] = (
        2.0 * (total + dot(pick[:, border_rows:], hub_back))
    ).astype(BF)

    wait_bytes(out_border.at[pl.ds(0, others)], send_sem.at[BORDER])
    wait_bytes(line_hub.at[pl.ds(0, n_hi - 1)], send_sem.at[HUB_LINE])
    wait_bytes(in_hub.at[pl.ds(0, n_q - 1)], send_sem.at[HUB_NEAR])
    wait_bytes(back_border.at[pl.ds(0, others)], send_sem.at[BACK_BORDER])
    wait_bytes(back_hub.at[pl.ds(0, n_q - 1)], send_sem.at[BACK_NEAR])
    wait_bytes(line_back.at[pl.ds(0, n_hi - 1)], send_sem.at[BACK_LINE])
    for which in range(CUTS):
        wait_bytes(part.at[pl.ds(which * cut, near_rows)], send_sem.at[SCATTER + which])
        wait_bytes(across.at[pl.ds(which * n_hi * piece, line_rows)], send_sem.at[CROSS + which])
    for which in range(CUTS):
        wait_bytes(out_ref.at[pl.ds(which * cut, near_rows)], recv_sem.at[GATHER + which])
        wait_bytes(part.at[pl.ds(which * cut, near_rows)], send_sem.at[GATHER + which])


def local(features, neighbours, send_rows, block_counts, hub_rows, w_self, w_nbr, cotangent):
    nodes, width = features.shape
    n_member = lax.axis_size("member")
    n_group = lax.axis_size("group")
    block = send_rows.shape[1]
    hubs = hub_rows.shape[1]
    owners = n_group * n_member
    hub2 = 2 * hubs
    low = max(1, 8 // n_group)
    n_q = n_group * low
    n_hi = n_member // low
    piece = 2 * width // (CUTS * n_q)
    half = width // 2
    border_rows = n_member * block
    table_rows = nodes + border_rows + owners * hub2
    border = pltpu.VMEM((border_rows, width), BF)
    hub_line = pltpu.VMEM((n_hi, hub2, half), BF)
    hub_all = pltpu.VMEM((n_q, n_hi, hub2, half), BF)
    pair = pltpu.VMEM((2 * width, width), BF)
    result = pl.pallas_call(
        functools.partial(kernel, n_group, n_member, low, block, hubs),
        out_shape=pltpu.VMEM((2 * width + nodes, width), BF),
        in_specs=[pl.BlockSpec(memory_space=pltpu.HBM)] * 8,
        out_specs=pl.BlockSpec(memory_space=pltpu.VMEM),
        scratch_shapes=[
            pltpu.VMEM((nodes, width), BF),
            pltpu.VMEM((neighbours.shape[1], nodes), jnp.int32),
            pltpu.VMEM(send_rows.shape, jnp.int32),
            pltpu.VMEM((1, n_member), jnp.int32),
            pltpu.VMEM(hub_rows.shape, jnp.int32),
            pltpu.VMEM((width, width), BF),
            pltpu.VMEM((width, width), BF),
            pltpu.VMEM((nodes, width), BF),
            pltpu.SemaphoreType.DMA((8,)),
            pltpu.VMEM((table_rows, nodes), BF),
            pltpu.VMEM((nodes, table_rows), BF),
            border,
            border,
            pltpu.VMEM((hub2, half), BF),
            hub_line,
            hub_all,
            border,
            border,
            hub_all,
            hub_all,
            hub_line,
            hub_line,
            pair,
            pair,
            pltpu.VMEM((CUTS * piece, width), BF),
            pltpu.VMEM((CUTS * n_hi * piece, width), BF),
            pltpu.VMEM((CUTS * piece, width), BF),
            pltpu.SemaphoreType.DMA((SEMS,)),
            pltpu.SemaphoreType.DMA((SEMS,)),
        ],
        compiler_params=pltpu.CompilerParams(
            collective_id=0, has_side_effects=True, vmem_limit_bytes=60 * 1024 * 1024
        ),
    )(
        features,
        neighbours.T,
        send_rows,
        block_counts.reshape(1, -1),
        hub_rows,
        w_self,
        w_nbr,
        cotangent,
    )
    scale = 1.0 / math.sqrt(nodes * owners)
    grad_self = result[:width].astype(F32) * scale
    grad_nbr = result[width : 2 * width].astype(F32) * scale
    grad_feat = (result[2 * width :].astype(F32) * 0.5).astype(BF)
    return (grad_self, grad_nbr, grad_feat)


def solution(mesh):
    in_specs = (
        P(("group", "member"), None),
        P(("group", "member"), None),
        P(("group", "member"), None),
        P(("group", "member")),
        P(("group", "member"), None),
        P(),
        P(),
        P(("group", "member"), None),
    )
    out_specs = (P(), P(), P(("group", "member"), None))
    return jax.shard_map(local, mesh=mesh, in_specs=in_specs, out_specs=out_specs, check_vma=False)
```

```python
import functools
import math

import jax
import jax.numpy as jnp
from jax import lax
from jax.experimental import pallas as pl
from jax.experimental.pallas import tpu as pltpu
from jax.sharding import PartitionSpec as P

MESH = pl.DeviceIdType.MESH
BF = jnp.bfloat16
F32 = jnp.float32
CHUNK = 128
BORDER, HUB_LINE, HUB_NEAR, BACK_BORDER, BACK_NEAR, BACK_LINE = range(6)
SCATTER, CROSS, GATHER = 6, 8, 10
SEMS = 12


def dot(a, b):
    return jnp.dot(a, b, preferred_element_type=F32)


def dot_tn(a, b):
    return lax.dot_general(a, b, (((0,), (0,)), ((), ())), preferred_element_type=F32)


def dot_nt(a, b):
    return lax.dot_general(a, b, (((1,), (1,)), ((), ())), preferred_element_type=F32)


def split(value):
    high = value.astype(BF)
    return high, (value - high.astype(F32)).astype(BF)


def wait_bytes(ref, sem):
    pltpu.make_async_copy(ref, ref, sem).wait()


def select_rows(n_member, block, send_rows, counts):
    lanes = n_member * block
    lane = lax.broadcasted_iota(jnp.int32, (n_member, lanes), 1)
    peer = lax.broadcasted_iota(jnp.int32, (n_member, lanes), 0)
    own = lane // block == peer
    slot = lax.broadcasted_iota(jnp.int32, (block, lanes), 0)
    slot_lane = lax.broadcasted_iota(jnp.int32, (block, lanes), 1) % block
    expand = jnp.where(slot == slot_lane, 1.0, 0.0).astype(BF)
    spread_rows = dot(send_rows.astype(F32).astype(BF), expand)
    row = jnp.sum(jnp.where(own, spread_rows, 0.0), axis=0, keepdims=True)
    repeat = jnp.where(own, 1.0, 0.0).astype(BF)
    counts = jnp.broadcast_to(counts.astype(F32), (8, n_member)).astype(BF)
    live = dot(counts, repeat)[:1].astype(jnp.int32)
    lane = lax.broadcasted_iota(jnp.int32, (1, lanes), 1)
    return jnp.where(lane % block < live, row.astype(jnp.int32), -1)


def select_hubs(hubs, hub_rows):
    lane = lax.broadcasted_iota(jnp.int32, (hubs, 128), 1)
    hub = lax.broadcasted_iota(jnp.int32, (hubs, 128), 0)
    repeat = jnp.where(lane % hubs == hub, 1.0, 0.0).astype(BF)
    wide = jnp.broadcast_to(hub_rows.astype(F32), (8, hubs)).astype(BF)
    row = dot(wide, repeat)[:1].astype(jnp.int32)
    lane = lax.broadcasted_iota(jnp.int32, (1, 128), 1)
    return jnp.where(lane < 4 * hubs, row, -1)


def kernel(
    n_group,
    n_member,
    low,
    cuts,
    block,
    hubs,
    feat_hbm,
    nbr_hbm,
    rows_hbm,
    counts_hbm,
    hubs_hbm,
    wself_hbm,
    wnbr_hbm,
    cot_hbm,
    out_ref,
    feat_ref,
    nbr_ref,
    rows_ref,
    counts_ref,
    hubs_ref,
    wself_ref,
    wnbr_ref,
    cot_ref,
    load_sem,
    onehot,
    onehot_t,
    out_border,
    in_border,
    out_hub,
    line_hub,
    in_hub,
    back_border,
    ret_border,
    back_hub,
    ret_hub,
    line_back,
    line_ret,
    part,
    scattered,
    mine,
    across,
    reduced,
    landed,
    send_sem,
    recv_sem,
):
    nodes, width = feat_ref.shape
    half = width // 2
    fan = nbr_ref.shape[0]
    owners = n_group * n_member
    hub2 = 2 * hubs
    border_rows = n_member * block
    hub_base = nodes + border_rows
    g = lax.axis_index("group")
    m = lax.axis_index("member")
    hi, lo = lax.div(m, low), lax.rem(m, low)
    n_hi = n_member // low
    n_q = n_group * low
    q = g * low + lo
    piece = 2 * width // (cuts * n_q)
    cut = n_q * piece

    loads = [
        pltpu.make_async_copy(src, dst, load_sem.at[index])
        for index, (src, dst) in enumerate(
            (
                (rows_hbm, rows_ref),
                (counts_hbm, counts_ref),
                (hubs_hbm, hubs_ref),
                (feat_hbm, feat_ref),
                (nbr_hbm, nbr_ref),
                (wself_hbm, wself_ref),
                (wnbr_hbm, wnbr_ref),
                (cot_hbm, cot_ref),
            )
        )
    ]
    for load in loads:
        load.start()

    def loop(count, body):
        lax.fori_loop(1, count, lambda step, carry: (body(step), carry)[1], 0)

    def member(step):
        down, up = n_member - step, step - 1
        down = jnp.where(down > m, down, down - 1)
        up = jnp.where(up < m, up, up + 1)
        peer = jnp.where(m < n_member // 2, down, up)
        return peer, (g, peer)

    def near(step):
        peer = lax.rem(q + step, n_q)
        return peer, (lax.div(peer, low), hi * low + lax.rem(peer, low))

    def line(step):
        peer = lax.rem(hi + step, n_hi)
        return peer, (g, peer * low + lo)

    barrier = pltpu.get_barrier_semaphore()

    def greet(device):
        pl.semaphore_signal(barrier, inc=1, device_id=device, device_id_type=MESH)

    loop(n_member, lambda step: greet(member(step)[1]))
    for step in range(1, n_group):
        for other in range(low):
            greet((lax.rem(g + step, n_group), hi * low + other))

    def copy(src, dst, which, device):
        pltpu.make_async_remote_copy(
            src_ref=src,
            dst_ref=dst,
            send_sem=send_sem.at[which],
            recv_sem=recv_sem.at[which],
            device_id=device,
            device_id_type=MESH,
        ).start()

    def rows(start, count):
        return pl.ds(pl.multiple_of(start * count, count), count)

    def to_members(src, dst, which):
        def body(step):
            peer, device = member(step)
            copy(src.at[rows(peer, block)], dst.at[rows(m, block)], which, device)

        loop(n_member, body)
        dst[rows(m, block), :] = src[rows(m, block), :]

    for load in loads[:3]:
        load.wait()
    sel_rows = select_rows(n_member, block, rows_ref[...], counts_ref[...])
    sel = jnp.concatenate([sel_rows, select_hubs(hubs, hubs_ref[...])], axis=1)
    row_of = lax.broadcasted_iota(jnp.int32, (nodes, border_rows + 128), 0)
    pick = jnp.where(row_of == sel, 1.0, 0.0).astype(BF)
    loads[3].wait()
    feat = feat_ref[...]
    picked = dot_tn(pick, feat)
    out_border[...] = picked[:border_rows].astype(BF)
    hub_wide = picked[border_rows : border_rows + hub2]
    lane_row = lax.broadcasted_iota(jnp.int32, (hub2, half), 0)
    out_hub[...] = jnp.where(lane_row < hubs, hub_wide[:, :half], hub_wide[:, half:]).astype(BF)

    pl.semaphore_wait(barrier, n_member - 1 + (n_group - 1) * low)

    loop(n_hi, lambda step: copy(out_hub, line_hub.at[hi], HUB_LINE, line(step)[1]))
    line_hub[hi] = out_hub[...]
    to_members(out_border, in_border, BORDER)

    for load in loads[4:]:
        load.wait()

    def count(names):
        names = jnp.concatenate([names] * (nodes // 128), axis=1)
        total = jnp.zeros((CHUNK, nodes), F32)
        for sample in range(fan):
            total = total + jnp.where(names == nbr_ref[sample : sample + 1, :], 1.0, 0.0)
        return total

    def chunk_names(index):
        return lax.broadcasted_iota(jnp.int32, (CHUNK, 128), 0) + index * CHUNK

    def store(index, total):
        onehot[rows(index, CHUNK), :] = total.astype(BF)
        onehot_t[:, rows(index, CHUNK)] = total.T.astype(BF)

    def fill(index, carry):
        row = chunk_names(index)
        hub_row = row - hub_base
        slab = lax.div(hub_row, hub2)
        near_id = lax.div(slab, n_hi)
        owner = (
            lax.div(near_id, low) * n_member + lax.rem(slab, n_hi) * low + lax.rem(near_id, low)
        )
        hub_name = hub_base + owner * hubs + lax.rem(hub_row, hubs)
        store(index, count(jnp.where(row < hub_base, row, hub_name)))
        return carry

    early = nodes // CHUNK
    lax.fori_loop(0, early, fill, 0)

    if n_hi > 1:
        wait_bytes(line_hub.at[pl.ds(0, n_hi - 1)], recv_sem.at[HUB_LINE])
    loop(n_q, lambda step: copy(line_hub, in_hub.at[q], HUB_NEAR, near(step)[1]))
    in_hub[q] = line_hub[...]

    lax.fori_loop(early, onehot.shape[0] // CHUNK, fill, 0)
    pre_self = dot(feat, wself_ref[...])
    agg_sum = dot(onehot_t[:, :nodes], feat)
    feat_t = feat.astype(F32).T.astype(BF)

    wait_bytes(in_hub.at[pl.ds(0, n_q - 1)], recv_sem.at[HUB_NEAR])
    hub_half = lax.broadcasted_iota(jnp.int32, (owners * hub2, half), 0) % hub2 < hubs
    hub_rows = in_hub[...].astype(F32).reshape(owners * hub2, half)
    zero = jnp.zeros((), F32)
    hub_table = jnp.concatenate(
        [jnp.where(hub_half, hub_rows, zero), jnp.where(hub_half, zero, hub_rows)], axis=1
    ).astype(BF)
    agg_sum = agg_sum + dot(onehot_t[:, hub_base:], hub_table)
    others = (n_member - 1) * block
    wait_bytes(in_border.at[pl.ds(0, others)], recv_sem.at[BORDER])
    agg_sum = agg_sum + dot(onehot_t[:, nodes:hub_base], in_border[...])
    agg = (agg_sum * (1.0 / fan)).astype(BF)

    pre = pre_self + dot(agg, wnbr_ref[...])
    sigma = 0.5 * jnp.tanh(0.5 * pre) + 0.5
    dpre = (cot_ref[...].astype(F32) * sigma * (1.0 + pre * (1.0 - sigma))).astype(BF)

    def scatter(which):
        def body(step):
            peer, device = near(step)
            copy(
                part.at[rows(which * n_q + peer, piece)],
                scattered.at[rows(which * n_q + q, piece)],
                SCATTER + which,
                device,
            )

        loop(n_q, body)
        own = rows(which * n_q + q, piece)
        scattered[own, :] = part[own, :]

    part[:width, :] = dot(feat_t, dpre).astype(BF)
    if cuts == 2:
        scatter(0)
    part[width:, :] = dot_tn(agg, dpre).astype(BF)
    scatter(cuts - 1)

    dagg = dot_nt(dpre, wnbr_ref[...]) * (1.0 / fan)
    dagg = dagg.astype(BF)

    def spread(start, stop):
        return dot(onehot[start:stop, :], dagg)

    hub_wide = spread(hub_base, hub_base + owners * hub2)
    hub_wide = jnp.where(hub_half, hub_wide[:, :half], hub_wide[:, half:])
    back_hub[...] = hub_wide.reshape(n_q, n_hi, hub2, half).astype(BF)

    def send_back(step):
        peer, device = near(step)
        copy(back_hub.at[peer], ret_hub.at[q], BACK_NEAR, device)

    loop(n_q, send_back)
    ret_hub[q] = back_hub[q]
    back_border[...] = spread(nodes, hub_base).astype(BF)
    to_members(back_border, ret_border, BACK_BORDER)

    near_rows = (n_q - 1) * piece
    line_rows = (n_hi - 1) * piece

    def cross(which):
        wait_bytes(scattered.at[pl.ds(which * cut, near_rows)], recv_sem.at[SCATTER + which])
        summed = jnp.zeros((piece, width), F32)
        for index in range(n_q):
            start = which * cut + index * piece
            summed = summed + scattered[start : start + piece, :].astype(F32)
        source = mine.at[pl.ds(which * piece, piece)]
        source[...] = summed.astype(BF)
        slot = rows(which * n_hi + hi, piece)
        loop(n_hi, lambda step: copy(source, across.at[slot], CROSS + which, line(step)[1]))
        across[slot, :] = source[...]

    for which in range(cuts):
        cross(which)

    total = dot_nt(dpre, wself_ref[...]) + spread(0, nodes)

    wait_bytes(ret_hub.at[pl.ds(0, n_q - 1)], recv_sem.at[BACK_NEAR])
    line_back[...] = jnp.sum(ret_hub[...].astype(F32), axis=0).astype(BF)

    def send_line(step):
        peer, device = line(step)
        copy(line_back.at[peer], line_ret.at[hi], BACK_LINE, device)

    loop(n_hi, send_line)
    line_ret[hi] = line_back[hi]

    def gather(which):
        first = which * n_hi
        if n_hi > 1:
            wait_bytes(across.at[pl.ds(first * piece, line_rows)], recv_sem.at[CROSS + which])
        summed = lax.fori_loop(
            0,
            n_hi,
            lambda index, carry: carry + across[rows(first + index, piece), :].astype(F32),
            jnp.zeros((piece, width), F32),
            unroll=n_hi <= 16,
        )
        source = reduced.at[pl.ds(which * piece, piece)]
        source[...] = summed.astype(BF)
        slot = rows(which * n_q + q, piece)
        loop(n_q, lambda step: copy(source, landed.at[slot], GATHER + which, near(step)[1]))
        landed[slot, :] = source[...]

    for which in range(cuts):
        gather(which)

    wait_bytes(ret_border.at[pl.ds(0, others)], recv_sem.at[BACK_BORDER])
    total = total + dot(pick[:, :border_rows], ret_border[...])
    if n_hi > 1:
        wait_bytes(line_ret.at[pl.ds(0, n_hi - 1)], recv_sem.at[BACK_LINE])
    hub_sum = jnp.sum(line_ret[...].astype(F32), axis=0)
    top = lane_row < hubs
    hub_sum = jnp.concatenate(
        [jnp.where(top, hub_sum, zero), jnp.where(top, zero, hub_sum)], axis=1
    )
    hub_high, hub_low = split(hub_sum)
    hub_back = jnp.concatenate(
        [
            hub_high.astype(F32),
            hub_low.astype(F32),
            jnp.zeros((128 - 2 * hub2, width), F32),
        ],
        axis=0,
    ).astype(BF)
    out_ref[2 * width :, :] = 2.0 * (total + dot(pick[:, border_rows:], hub_back))

    wait_bytes(out_border.at[pl.ds(0, others)], send_sem.at[BORDER])
    if n_hi > 1:
        wait_bytes(line_hub.at[pl.ds(0, n_hi - 1)], send_sem.at[HUB_LINE])
    wait_bytes(in_hub.at[pl.ds(0, n_q - 1)], send_sem.at[HUB_NEAR])
    wait_bytes(back_border.at[pl.ds(0, others)], send_sem.at[BACK_BORDER])
    wait_bytes(back_hub.at[pl.ds(0, n_q - 1)], send_sem.at[BACK_NEAR])
    if n_hi > 1:
        wait_bytes(line_back.at[pl.ds(0, n_hi - 1)], send_sem.at[BACK_LINE])
    for which in range(cuts):
        wait_bytes(part.at[pl.ds(which * cut, near_rows)], send_sem.at[SCATTER + which])
        if n_hi > 1:
            wait_bytes(
                across.at[pl.ds(which * n_hi * piece, line_rows)], send_sem.at[CROSS + which]
            )
    for which in range(cuts):
        wait_bytes(landed.at[pl.ds(which * cut, near_rows)], recv_sem.at[GATHER + which])
        span = slice(which * cut, (which + 1) * cut)
        out_ref[span, :] = landed[span, :].astype(F32)
        wait_bytes(part.at[pl.ds(which * cut, near_rows)], send_sem.at[GATHER + which])


def local(features, neighbours, send_rows, block_counts, hub_rows, w_self, w_nbr, cotangent):
    nodes, width = features.shape
    n_member = lax.axis_size("member")
    n_group = lax.axis_size("group")
    block = send_rows.shape[1]
    hubs = hub_rows.shape[1]
    owners = n_group * n_member
    hub2 = 2 * hubs
    low, cuts = max(1, 8 // n_group), 1
    n_q = n_group * low
    n_hi = n_member // low
    piece = 2 * width // (cuts * n_q)
    half = width // 2
    border_rows = n_member * block
    table_rows = nodes + border_rows + owners * hub2
    border = pltpu.VMEM((border_rows, width), BF)
    hub_line = pltpu.VMEM((n_hi, hub2, half), BF)
    hub_all = pltpu.VMEM((n_q, n_hi, hub2, half), BF)
    pair = pltpu.VMEM((2 * width, width), BF)
    result = pl.pallas_call(
        functools.partial(kernel, n_group, n_member, low, cuts, block, hubs),
        out_shape=pltpu.VMEM((2 * width + nodes, width), F32),
        in_specs=[pl.BlockSpec(memory_space=pltpu.HBM)] * 8,
        out_specs=pl.BlockSpec(memory_space=pltpu.VMEM),
        scratch_shapes=[
            pltpu.VMEM((nodes, width), BF),
            pltpu.VMEM((neighbours.shape[1], nodes), jnp.int32),
            pltpu.VMEM(send_rows.shape, jnp.int32),
            pltpu.VMEM((1, n_member), jnp.int32),
            pltpu.VMEM(hub_rows.shape, jnp.int32),
            pltpu.VMEM((width, width), BF),
            pltpu.VMEM((width, width), BF),
            pltpu.VMEM((nodes, width), BF),
            pltpu.SemaphoreType.DMA((8,)),
            pltpu.VMEM((table_rows, nodes), BF),
            pltpu.VMEM((nodes, table_rows), BF),
            border,
            border,
            pltpu.VMEM((hub2, half), BF),
            hub_line,
            hub_all,
            border,
            border,
            hub_all,
            hub_all,
            hub_line,
            hub_line,
            pair,
            pair,
            pltpu.VMEM((cuts * piece, width), BF),
            pltpu.VMEM((cuts * n_hi * piece, width), BF),
            pltpu.VMEM((cuts * piece, width), BF),
            pair,
            pltpu.SemaphoreType.DMA((SEMS,)),
            pltpu.SemaphoreType.DMA((SEMS,)),
        ],
        compiler_params=pltpu.CompilerParams(
            collective_id=0, has_side_effects=True, vmem_limit_bytes=60 * 1024 * 1024
        ),
    )(
        features,
        neighbours.T,
        send_rows,
        block_counts.reshape(1, -1),
        hub_rows,
        w_self,
        w_nbr,
        cotangent,
    )
    scale = 1.0 / math.sqrt(nodes * owners)
    grad_self = result[:width] * scale
    grad_nbr = result[width : 2 * width] * scale
    return (grad_self, grad_nbr, (0.5 * result[2 * width :]).astype(BF))


def solution(mesh):
    in_specs = (
        P(("group", "member"), None),
        P(("group", "member"), None),
        P(("group", "member"), None),
        P(("group", "member")),
        P(("group", "member"), None),
        P(),
        P(),
        P(("group", "member"), None),
    )
    out_specs = (P(), P(), P(("group", "member"), None))
    return jax.shard_map(local, mesh=mesh, in_specs=in_specs, out_specs=out_specs, check_vma=False)
```
